256 devices in a mesh: boxes: 128 (over z, x, y), dirs: 2 (over core).
Axes of the slice: x: 4, y: 4, z: 8, core: 2. Of those that a mesh axis runs over, the one named last changes fastest.
Arguments:
- points: bfloat16 [4096, 2, 192], P('boxes', 'dirs'), may hold values from -1 to 1
- charges: bfloat16 [4096, 2, 4, 128], P('boxes', 'dirs'), may hold values from -6 to 6
- near_box: int32 [4096, 27], P('boxes'), may hold values from 0 to 4095, as said below
- near_code: int32 [4096, 27], P('boxes'), may hold values from 0 to 26
- send_box: int32 [16384, 16], P('boxes'), may hold values from 0 to 31
- far_slot: int32 [4096, 128], P('boxes'), may hold values from 0 to 2047, as said below
- far_direction: int32 [4096, 128], P('boxes'), may hold values from 0 to 15
- coarse_source: int32 [512, 32], P('boxes'), may hold values from 0 to 511
- coarse_direction: int32 [512, 32], P('boxes'), may hold values from 0 to 15
- leaf_translate: bfloat16 [16, 256, 256], P('dirs'), may hold values from -0.5 to 0.5
- coarse_translate: bfloat16 [16, 256, 256], P('dirs'), may hold values from -0.375 to 0.375
- child_to_parent: bfloat16 [8, 256, 256], replicated, may hold values from -0.375 to 0.375
- parent_to_child: bfloat16 [8, 256, 256], replicated, may hold values from -0.1875 to 0.1875
Outputs:
- potential: bfloat16 [4096, 2, 4, 128], P('boxes', 'dirs')
The draws below stay inside these ranges and needn't reach their ends.
Inputs may be any that keep to these rules, and one draw needn't show every extreme that they name: `near_box`: every entry names a box at most 8 places from the box itself along the curve; each box has entries 8 places before and after it wherever such boxes exist. `far_slot`: A value s * 16 + c names slot c of the buffer that device s sends to the device holding the box; where c >= 7, s is at most 2 devices from that device. Every slot allowed so is named by some entry of that device's boxes.
All inputs are finite; a program needn't handle non-finite values.
Results may differ from the reference program's by a relative error of at most 0.009.
Values may be sent and summed in bfloat16 or wider, within the bound.
A program may use at most 64 MiB of HBM per device.

```python
import jax
import jax.numpy as jnp
from jax import lax

BOX_DEV = 32
PTS = 128
EQ = 128
DIRS = 16
RHS = 4
NEAR = 27
LIST = 128
CLIST = 32
CAP = 16
CAP_FAR = 7
REACH = 2
HB = 8
NBOX = 4096
PAR_DEV = 4
NPAR = 512
PH = 64
N_BOXES = 128
N_DIRS = 2


def draw_near_box(key, part):
    key = jax.random.fold_in(key, 3)
    strides = jax.random.randint(key, (NBOX, NEAR), -HB, HB + 1).astype(jnp.int32)
    column = jnp.arange(NEAR, dtype=jnp.int32)[None, :]
    strides = jnp.where(column == 1, -HB, jnp.where(column == 2, HB, strides))
    neighbours = jnp.arange(NBOX, dtype=jnp.int32)[:, None] + strides
    return jnp.clip(neighbours, 0, NBOX - 1).astype(jnp.int32)


def compact_slots(usable):
    flat_ids = jnp.arange(N_BOXES * CAP, dtype=jnp.int32)
    ranking = jnp.cumsum(usable.astype(jnp.int32)) - 1
    count = jnp.sum(usable.astype(jnp.int32))
    where_to = jnp.where(usable, ranking, N_BOXES * CAP).astype(jnp.int32)
    ordered = jnp.zeros((N_BOXES * CAP,), jnp.int32).at[where_to].set(flat_ids, mode='drop')
    return (ordered, count)


def draw_far_slot(key, part):
    key = jax.random.fold_in(key, 7)
    senders = jnp.arange(N_BOXES, dtype=jnp.int32)
    columns = jnp.arange(CAP, dtype=jnp.int32)
    entries = BOX_DEV * LIST

    def one_device(target):
        nearby = jnp.abs(senders - target) <= REACH
        near_ok = (nearby[:, None] & (columns[None, :] >= 0)).reshape(-1)
        far_ok = ((~nearby)[:, None] & (columns[None, :] < CAP_FAR)).reshape(-1)
        all_list, live_count = compact_slots(near_ok | far_ok)
        near_list, near_count = compact_slots(near_ok)
        far_list, far_count = compact_slots(far_ok)
        device_key = jax.random.fold_in(key, target)
        key_order, key_kind, key_near, key_far = jax.random.split(device_key, 4)
        order = jax.random.permutation(key_order, entries).astype(jnp.int32)
        pick_near = jax.random.randint(key_kind, (entries,), 0, 8) < 4
        near_pick = near_list[jax.random.randint(key_near, (entries,), 0, near_count)]
        far_pick = far_list[jax.random.randint(key_far, (entries,), 0, far_count)]
        extra = jnp.where(pick_near, near_pick, far_pick)
        covered = all_list[jnp.minimum(order, N_BOXES * CAP - 1)]
        values = jnp.where(order < live_count, covered, extra)
        return values.reshape(BOX_DEV, LIST)
    return jax.vmap(one_device)(senders).reshape(NBOX, LIST).astype(jnp.int32)


def plant(drawn, key, low, largest):
    dims = drawn.shape
    spot = [jax.random.randint(jax.random.fold_in(key, axis), (), 0, dims[axis]) for axis in range(len(dims))]
    drawn = drawn.at[tuple(spot)].set(low)
    longest = dims.index(max(dims))
    spot[longest] = (spot[longest] + 1) % dims[longest]
    return drawn.at[tuple(spot)].set(largest)


def block_levels(rng, dims, cuts, low, largest):
    factor_of = 1.0
    for position, blocks in cuts:
        draws = jax.random.uniform(jax.random.fold_in(jax.random.fold_in(rng, 6), position), (blocks,), jnp.float32, low / len(cuts), largest / len(cuts))
        factor_of = factor_of * jnp.repeat(jnp.exp(draws), dims[position] // blocks).reshape((-1,) + (1,) * (len(dims) - 1 - position))
    return factor_of


def gaussian(rng, dims, scale, bound, pieces=(), kind=jnp.bfloat16):
    drawn = jax.random.normal(rng, dims, jnp.float32) * scale
    if len(pieces) > 0:
        drawn = block_levels(rng, dims, pieces, -0.22, 0.18) * drawn
    return jnp.clip(drawn, min=-bound, max=bound).astype(kind)


def setup_inputs(seed: int = 0) -> dict:
    key_list = jax.random.split(jax.random.key(seed), 14)
    return {
        "points": jnp.clip(jax.random.uniform(key_list[0], (NBOX, N_DIRS, 3 * PH), jnp.float32, -1.0, 1.0) * block_levels(key_list[0], (NBOX, N_DIRS, 3 * PH), ((0, 128), (1, 2)), -0.4, 0.0), -1.0, 1.0).astype(jnp.bfloat16),
        "charges": gaussian(key_list[1], (NBOX, N_DIRS, RHS, 2 * PH), 1.0, 6.0, ((0, 128), (1, 2))),
        "near_box": draw_near_box(jax.random.fold_in(key_list[13], 71), 0),
        "near_code": plant(jax.random.randint(key_list[3], (NBOX, NEAR), 0, 27), jax.random.fold_in(key_list[3], 1), 0, 26).astype(jnp.int32),
        "send_box": plant(jax.random.randint(key_list[4], (N_BOXES * N_BOXES, CAP), 0, BOX_DEV), jax.random.fold_in(key_list[4], 1), 0, BOX_DEV - 1).astype(jnp.int32),
        "far_slot": draw_far_slot(jax.random.fold_in(key_list[13], 71), 0),
        "far_direction": plant(jax.random.randint(key_list[6], (NBOX, LIST), 0, DIRS), jax.random.fold_in(key_list[6], 1), 0, DIRS - 1).astype(jnp.int32),
        "coarse_source": plant(jax.random.randint(key_list[7], (NPAR, CLIST), 0, NPAR), jax.random.fold_in(key_list[7], 1), 0, NPAR - 1).astype(jnp.int32),
        "coarse_direction": plant(jax.random.randint(key_list[8], (NPAR, CLIST), 0, DIRS), jax.random.fold_in(key_list[8], 1), 0, DIRS - 1).astype(jnp.int32),
        "leaf_translate": gaussian(key_list[9], (DIRS, 2 * EQ, 2 * EQ), EQ ** -0.5, 0.5, ((0, 2),)),
        "coarse_translate": gaussian(key_list[10], (DIRS, 2 * EQ, 2 * EQ), (2 * EQ) ** -0.5, 0.375, ((0, 2),)),
        "child_to_parent": gaussian(key_list[11], (8, 2 * EQ, 2 * EQ), (2 * EQ) ** -0.5, 0.375),
        "parent_to_child": gaussian(key_list[12], (8, 2 * EQ, 2 * EQ), (8 * EQ) ** -0.5, 0.1875),
    }


wave_number = 3.0
smoothing = 0.0625
sphere_radius = 2.5
golden_turn = 2.399963229728653
four_pi = 12.566370614359172

def surface_points():
    ordinal = jnp.arange(EQ).astype(jnp.float32)
    height = 1.0 - (2.0 * ordinal + 1.0) / EQ
    radial = jnp.sqrt(1.0 - height * height)
    angles = ordinal * golden_turn
    return sphere_radius * jnp.stack([radial * jnp.cos(angles), radial * jnp.sin(angles), height])

def kernel_parts(squared):
    spread = jnp.sqrt(squared + smoothing)
    amplitude = 1.0 / (four_pi * spread)
    return ((amplitude * jnp.cos(wave_number * spread)).astype(jnp.bfloat16), (amplitude * jnp.sin(wave_number * spread)).astype(jnp.bfloat16))

def code_offsets(code_block):
    return 2.0 * jnp.stack([code_block // 9 - 1, code_block // 3 % 3 - 1, code_block % 3 - 1], axis=-1).astype(jnp.float32)

def box_positions(points):
    number = points.shape[0]
    halves = points.astype(jnp.float32).reshape(number, N_DIRS, 3, PH)
    return jnp.transpose(halves, (0, 2, 1, 3)).reshape(number, 3, PTS)

def box_charges(charges):
    number = charges.shape[0]
    halves = charges.astype(jnp.float32).reshape(number, N_DIRS, RHS, 2, PH)
    real_part = jnp.transpose(halves[:, :, :, 0, :], (0, 2, 1, 3)).reshape(number, RHS, PTS)
    imag_part = jnp.transpose(halves[:, :, :, 1, :], (0, 2, 1, 3)).reshape(number, RHS, PTS)
    return (real_part, imag_part)

def upward_kernel(block_pos):
    surface = surface_points()
    differences = surface[None, :, :, None] - block_pos[:, :, None, :]
    return kernel_parts(lax.optimization_barrier(jnp.sum(differences * differences, axis=1)))

def contract_up(kern, charge):
    return jnp.einsum('nep,nrp->nre', kern.astype(jnp.float32), charge)

def contract_down(kern, value):
    return jnp.einsum('nep,nre->nrp', kern.astype(jnp.float32), value)

def near_contract(kern, charge):
    return jnp.einsum('gkps,gkrs->grp', kern.astype(jnp.float32), charge)

def reference(points, charges, near_box, near_code, send_box, far_slot, far_direction, coarse_source, coarse_direction, leaf_translate, coarse_translate, child_to_parent, parent_to_child):
    positions = box_positions(points)
    charge_real, charge_imag = box_charges(charges)

    def upward_block(inputs):
        block_pos, block_real, block_imag = inputs
        kern_real, kern_imag = upward_kernel(block_pos)
        out_real = contract_up(kern_real, block_real) - contract_up(kern_imag, block_imag)
        out_imag = contract_up(kern_real, block_imag) + contract_up(kern_imag, block_real)
        return jnp.concatenate([out_real, out_imag], axis=-1).astype(jnp.bfloat16)
    outgoing = lax.map(upward_block, (positions.reshape(N_BOXES, BOX_DEV, 3, PTS), charge_real.reshape(N_BOXES, BOX_DEV, RHS, PTS), charge_imag.reshape(N_BOXES, BOX_DEV, RHS, PTS))).reshape(NBOX, RHS, 2 * EQ)
    grouped = outgoing.astype(jnp.float32).reshape(NPAR, 8, RHS, 2 * EQ)
    parent = jnp.einsum('cork,okj->crj', grouped, child_to_parent.astype(jnp.float32)).astype(jnp.bfloat16)
    send_table = send_box.reshape(N_BOXES, N_BOXES, CAP)
    all_directions = jnp.arange(DIRS).astype(jnp.int32)

    def device_block(ordinal):
        first_box = ordinal * BOX_DEV
        slot_ids = lax.dynamic_slice_in_dim(far_slot, first_box, BOX_DEV, 0)
        sender = slot_ids // CAP
        column = slot_ids % CAP
        send_rows = lax.dynamic_index_in_dim(send_table, ordinal, 1, keepdims=False)
        source = sender * BOX_DEV + send_rows[sender, column]
        gathered = outgoing[source].astype(jnp.float32)
        direction_ids = lax.dynamic_slice_in_dim(far_direction, first_box, BOX_DEV, 0)
        direction_hot = (direction_ids[:, :, None] == all_directions[None, None, :]).astype(jnp.float32)
        leaf_cone = jnp.einsum('bld,blrk->dbrk', direction_hot, gathered).astype(jnp.bfloat16)
        first_parent = ordinal * PAR_DEV
        parent_ids = lax.dynamic_slice_in_dim(coarse_source, first_parent, PAR_DEV, 0)
        parent_dirs = lax.dynamic_slice_in_dim(coarse_direction, first_parent, PAR_DEV, 0)
        parent_hot = (parent_dirs[:, :, None] == all_directions[None, None, :]).astype(jnp.float32)
        coarse_cone = jnp.einsum('cld,clrk->dcrk', parent_hot, parent[parent_ids].astype(jnp.float32)).astype(jnp.bfloat16)
        coarse_local = jnp.einsum('dcrk,dkj->crj', coarse_cone.astype(jnp.float32), coarse_translate.astype(jnp.float32)).astype(jnp.bfloat16)
        leaf_part = jnp.einsum('dbrk,dkj->brj', leaf_cone.astype(jnp.float32), leaf_translate.astype(jnp.float32))
        child_terms = jnp.einsum('crk,okj->corj', coarse_local.astype(jnp.float32), parent_to_child.astype(jnp.float32)).reshape(BOX_DEV, RHS, 2 * EQ)
        local_exp = (leaf_part + child_terms).astype(jnp.bfloat16)
        block_pos = lax.dynamic_slice_in_dim(positions, first_box, BOX_DEV, 0)
        kern_real, kern_imag = upward_kernel(block_pos)
        local_real = local_exp[:, :, :EQ].astype(jnp.float32)
        local_imag = local_exp[:, :, EQ:].astype(jnp.float32)
        far_real = contract_down(kern_real, local_real) - contract_down(kern_imag, local_imag)
        far_imag = contract_down(kern_imag, local_real) + contract_down(kern_real, local_imag)
        block_ids = lax.dynamic_slice_in_dim(near_box, first_box, BOX_DEV, 0)
        block_codes = lax.dynamic_slice_in_dim(near_code, first_box, BOX_DEV, 0)

        def near_group(inputs):
            targets, neighbour_ids, code_block = inputs
            source_pos = positions[neighbour_ids] + code_offsets(code_block)[..., None]
            differences = targets[:, None, :, :, None] - source_pos[:, :, :, None, :]
            kern_near_real, kern_near_imag = kernel_parts(lax.optimization_barrier(jnp.sum(differences * differences, axis=2)))
            source_real = charge_real[neighbour_ids]
            source_imag = charge_imag[neighbour_ids]
            near_real = near_contract(kern_near_real, source_real) - near_contract(kern_near_imag, source_imag)
            near_imag = near_contract(kern_near_imag, source_real) + near_contract(kern_near_real, source_imag)
            return (near_real, near_imag)
        groups = BOX_DEV // 8
        near_real, near_imag = lax.map(near_group, (block_pos.reshape(groups, 8, 3, PTS), block_ids.reshape(groups, 8, NEAR), block_codes.reshape(groups, 8, NEAR)))
        total_real = far_real + near_real.reshape(BOX_DEV, RHS, PTS)
        total_imag = far_imag + near_imag.reshape(BOX_DEV, RHS, PTS)

        def layout(values):
            return jnp.transpose(values.reshape(BOX_DEV, RHS, N_DIRS, PH), (0, 2, 1, 3))
        return jnp.concatenate([layout(total_real), layout(total_imag)], axis=-1).astype(jnp.bfloat16)
    result = lax.map(device_block, jnp.arange(N_BOXES).astype(jnp.int32))
    return result.reshape(NBOX, N_DIRS, RHS, 2 * PH)
```

```python
import functools
import math

import jax
import jax.numpy as jnp
import numpy as np
from jax import lax
from jax.experimental import pallas as pl
from jax.experimental.pallas import tpu as pltpu
from jax.sharding import PartitionSpec as P

PTS = 128
EQ = 128
DIRS = 16
RHS = 4
NEAR = 27
CAP = 16
HB = 8
PAR_DEV = 4


wave_number = 3.0
smoothing = 0.0625
sphere_radius = 2.5
golden_turn = 2.399963229728653
four_pi = 12.566370614359172


def with_halo(cells, sides, width):
    for axis, dim in sides:
        count = lax.axis_size(axis)
        ends = count - 1
        head = lax.slice_in_dim(cells, 0, width, axis=dim)
        tail = lax.slice_in_dim(cells, cells.shape[dim] - width, cells.shape[dim], axis=dim)
        cells = jnp.concatenate(
            [
                lax.ppermute(tail, axis, [(i, (i + 1) % count) for i in range(ends)]),
                cells,
                lax.ppermute(head, axis, [((i + 1) % count, i) for i in range(ends)]),
            ],
            axis=dim,
        )
    return cells


def surface_points():
    ordinal = jnp.arange(EQ).astype(jnp.float32)
    height = 1.0 - (2.0 * ordinal + 1.0) / EQ
    radial = jnp.sqrt(1.0 - height * height)
    angles = ordinal * golden_turn
    return sphere_radius * jnp.stack([radial * jnp.cos(angles), radial * jnp.sin(angles), height])


def kernel_parts(squared):
    spread = jnp.sqrt(squared + smoothing)
    amplitude = 1.0 / (four_pi * spread)
    return (
        (amplitude * jnp.cos(wave_number * spread)).astype(jnp.bfloat16),
        (amplitude * jnp.sin(wave_number * spread)).astype(jnp.bfloat16),
    )


def contract_up(kern, charge):
    return jnp.einsum("nep,nrp->nre", kern, charge, preferred_element_type=jnp.float32)


def contract_down(kern, value):
    return jnp.einsum("nep,nre->nrp", kern, value, preferred_element_type=jnp.float32)


FEATURES = 16
TURNS = 3.0 / (2.0 * math.pi)
COS_TERMS = (0.99999922, -19.73898252, 64.92872662, -85.27239703, 58.79403881, -21.07678228)
SIN_TERMS = (6.2830558, -41.33121431, 81.36681533, -74.47800473, 32.78140114)
AMPLITUDE = TURNS / four_pi


def split3(values):
    high = values.astype(jnp.bfloat16).astype(jnp.float32)
    rest = values - high
    middle = rest.astype(jnp.bfloat16).astype(jnp.float32)
    return high, middle, rest - middle


def horner(terms, z):
    total = z * (AMPLITUDE * terms[-1]) + AMPLITUDE * terms[-2]
    for term in terms[-3::-1]:
        total = total * z + AMPLITUDE * term
    return total


def wave(scaled):
    inverse = lax.rsqrt(scaled)
    phase = scaled * inverse
    phase = phase - jnp.round(phase)
    z = phase * phase
    return inverse * horner(COS_TERMS, z), (inverse * phase) * horner(SIN_TERMS, z)


def coordinates(first, second):
    return [
        jnp.concatenate([first[:, k * 64 : k * 64 + 64], second[:, k * 64 : k * 64 + 64]], axis=1)
        for k in range(3)
    ]


def source_features(coords):
    square = TURNS * TURNS * sum(c * c for c in coords)
    one = jnp.ones_like(square)
    return coords * 3 + list(split3(square)) + [one, one, one, jnp.zeros_like(one)]


def target_features(coords):
    scale = TURNS * TURNS
    square = scale * (sum(c * c for c in coords) + smoothing)
    one = jnp.ones_like(square)
    parts = [split3(-2.0 * scale * c) for c in coords]
    rows = [parts[k][i] for i in range(3) for k in range(3)]
    return rows + [one, one, one] + list(split3(square)) + [jnp.zeros_like(one)]


def near_kernel(box_ref, code_ref, pos_ref, charge_ref, out_ref, rows_ref, source_ref, target_ref, dense_ref):
    half_boxes = out_ref.shape[0]
    boxes = pos_ref.shape[1]
    coords = coordinates(pos_ref[0].astype(jnp.float32), pos_ref[1].astype(jnp.float32))
    for f, row in enumerate(source_features(coords)):
        rows_ref[pl.ds(f, boxes, stride=FEATURES), :] = row

    def turn(j, carry):
        tile = rows_ref[pl.ds(pl.multiple_of(j * FEATURES, FEATURES), FEATURES), :]
        source_ref[pl.ds(pl.multiple_of(j * PTS, PTS), PTS), :] = tile.T.astype(jnp.bfloat16)
        return carry

    lax.fori_loop(0, boxes, turn, 0)
    mine = [c[HB : HB + half_boxes] for c in coords]
    for code in range(27):
        offset = (2.0 * (code // 9 - 1), 2.0 * (code // 3 % 3 - 1), 2.0 * (code % 3 - 1))
        moved = [c - o for c, o in zip(mine, offset)]
        for f, row in enumerate(target_features(moved)):
            target_ref[pl.ds(code * half_boxes * FEATURES + f, half_boxes, stride=FEATURES), :] = row

    lane = lax.broadcasted_iota(jnp.int32, (4, 128), 1)
    sign = jnp.where(lane < 64, 1.0, -1.0)

    def weigh(j, carry):
        parts = []
        for h in range(2):
            q = charge_ref[h, j].astype(jnp.float32)
            parts.append(jnp.concatenate([q * sign, pltpu.roll(q, 64, 1)], axis=0))
        both = jnp.concatenate(parts, axis=1)
        dense_ref[pl.ds(pl.multiple_of(j * 16, 16), 16), :] = jnp.concatenate(
            [both, jnp.zeros_like(both)], axis=0
        ).astype(jnp.bfloat16)
        return carry

    lax.fori_loop(0, boxes, weigh, 0)

    def one_box(b, carry):
        def group(g, total):
            for i in range(9):
                n = g * 9 + i
                j = box_ref[b, n]
                code = code_ref[b, n]
                y = source_ref[pl.ds(pl.multiple_of(j * PTS, PTS), PTS), :]
                x = target_ref[
                    pl.ds(pl.multiple_of((code * half_boxes + b) * FEATURES, FEATURES), FEATURES), :
                ].astype(jnp.bfloat16)
                real, imag = wave(jnp.dot(y, x, preferred_element_type=jnp.float32))
                real, imag = real.astype(jnp.bfloat16), imag.astype(jnp.bfloat16)
                kern = jnp.concatenate([real[:64], imag[:64], real[64:], imag[64:]], axis=0)
                q = dense_ref[pl.ds(pl.multiple_of(j * 16, 16), 16), :]
                total = total + jnp.dot(q, kern, preferred_element_type=jnp.float32)
            return total

        total = lax.fori_loop(0, 3, group, jnp.zeros((16, PTS), jnp.float32))
        out_ref[b] = total[:8]
        return carry

    lax.fori_loop(0, half_boxes, one_box, 0)


def near_call(boxes_in, codes, positions, charges):
    half_boxes, boxes = boxes_in.shape[0], positions.shape[1]
    vmem = pl.BlockSpec(memory_space=pltpu.VMEM)
    smem = pl.BlockSpec(memory_space=pltpu.SMEM)
    return pl.pallas_call(
        near_kernel,
        out_shape=jax.ShapeDtypeStruct((half_boxes, 8, PTS), jnp.float32),
        in_specs=[smem, smem, vmem, vmem],
        out_specs=vmem,
        scratch_shapes=[
            pltpu.VMEM((boxes * FEATURES, 128), jnp.float32),
            pltpu.VMEM((boxes * PTS, FEATURES), jnp.bfloat16),
            pltpu.VMEM((27 * half_boxes * FEATURES, 128), jnp.float32),
            pltpu.VMEM((boxes * 16, 256), jnp.bfloat16),
        ],
        compiler_params=pltpu.CompilerParams(vmem_limit_bytes=40 * 1024 * 1024),
        cost_estimate=pl.CostEstimate(flops=10**9, bytes_accessed=10**6, transcendentals=0),
        name="near_field",
    )(boxes_in, codes, positions, charges)


def on_device(
    points,
    charges,
    near_box,
    near_code,
    send_box,
    far_slot,
    far_direction,
    coarse_source,
    coarse_direction,
    leaf_translate,
    coarse_translate,
    child_to_parent,
    parent_to_child,
):
    boxes_here = points.shape[0]
    halves = lax.axis_size("dirs")
    half_pts = points.shape[2] // 3
    rhs_half = RHS // halves
    device = lax.axis_index("boxes")
    peer_count = lax.axis_size("boxes")
    surface = surface_points()
    my_pos = points[:, 0, :].astype(jnp.float32).reshape(boxes_here, 3, half_pts)
    differences = surface[None, :, :, None] - my_pos[:, :, None, :]
    kern_real, kern_imag = kernel_parts(jnp.sum(differences * differences, axis=1))
    mine_real = charges[:, 0, :, :half_pts]
    mine_imag = charges[:, 0, :, half_pts:]
    part_real = contract_up(kern_real, mine_real) - contract_up(kern_imag, mine_imag)
    part_imag = contract_up(kern_real, mine_imag) + contract_up(kern_imag, mine_real)
    partial_value = jnp.concatenate([part_real, part_imag], axis=-1)
    outgoing = lax.psum_scatter(partial_value, "dirs", scatter_dimension=1, tiled=True).astype(
        jnp.bfloat16
    )
    grouped = outgoing.reshape(PAR_DEV, 8, rhs_half, 2 * EQ)
    parent = jnp.einsum(
        "cork,okj->crj", grouped, child_to_parent, preferred_element_type=jnp.float32
    ).astype(jnp.bfloat16)
    outbound = jnp.concatenate(
        [
            outgoing[send_box],
            jnp.broadcast_to(parent[None], (peer_count,) + parent.shape),
        ],
        axis=1,
    )
    received = lax.all_to_all(outbound, "boxes", split_axis=0, concat_axis=0, tiled=True)
    arrived = received[:, :CAP]
    gathered = arrived.reshape(peer_count * CAP, rhs_half * 2 * EQ)[far_slot]
    all_directions = jnp.arange(DIRS, dtype=jnp.int32)
    direction_hot = (far_direction[:, :, None] == all_directions[None, None, :]).astype(
        jnp.bfloat16
    )
    leaf_cone = (
        jnp.einsum("bld,blk->dbk", direction_hot, gathered, preferred_element_type=jnp.float32)
        .astype(jnp.bfloat16)
        .reshape(DIRS, boxes_here, rhs_half, 2 * EQ)
    )
    parent_hot = (coarse_direction[:, :, None] == all_directions[None, None, :]).astype(
        jnp.bfloat16
    )
    shard_rows = received[:, CAP:].reshape(peer_count * PAR_DEV, rhs_half, 2 * EQ)
    number = shard_rows.shape[0]
    wanted = (
        coarse_source[:, :, None] == jnp.arange(number, dtype=jnp.int32)[None, None, :]
    ).astype(jnp.bfloat16)
    weights = jnp.einsum(
        "cld,clj->dcj", parent_hot, wanted, preferred_element_type=jnp.float32
    ).astype(jnp.bfloat16)
    coarse_total = jnp.einsum(
        "dcj,jk->dck",
        weights,
        shard_rows.reshape(number, rhs_half * 2 * EQ),
        preferred_element_type=jnp.float32,
    )
    coarse_cone = coarse_total.astype(jnp.bfloat16).reshape(DIRS, PAR_DEV, rhs_half, 2 * EQ)
    leaf_table, coarse_table = (
        lax.all_gather(leaf_translate, "dirs", axis=0, tiled=True),
        lax.all_gather(coarse_translate, "dirs", axis=0, tiled=True),
    )
    coarse_local = jnp.einsum(
        "dcrk,dkj->crj", coarse_cone, coarse_table, preferred_element_type=jnp.float32
    ).astype(jnp.bfloat16)
    leaf_part = jnp.einsum(
        "dbrk,dkj->brj", leaf_cone, leaf_table, preferred_element_type=jnp.float32
    )
    child_terms = jnp.einsum(
        "crk,okj->corj", coarse_local, parent_to_child, preferred_element_type=jnp.float32
    ).reshape(boxes_here, rhs_half, 2 * EQ)
    local_half = (leaf_part + child_terms).astype(jnp.bfloat16)
    local_exp = lax.all_gather(local_half, "dirs", axis=1, tiled=True)
    local_real = local_exp[:, :, :EQ]
    local_imag = local_exp[:, :, EQ:]
    far_real = contract_down(kern_real, local_real) - contract_down(kern_imag, local_imag)
    far_imag = contract_down(kern_imag, local_real) + contract_down(kern_real, local_imag)
    all_points, all_charges = (
        lax.all_gather(points, "dirs", axis=1, tiled=True),
        lax.all_gather(charges, "dirs", axis=1, tiled=True),
    )
    sources = jnp.concatenate(
        [all_points, all_charges.reshape(boxes_here, halves, RHS * 2 * half_pts)], axis=-1
    )
    padded = with_halo(sources, (("boxes", 0),), HB)
    core = lax.axis_index("dirs")
    half_boxes = boxes_here // halves
    window = lax.dynamic_slice_in_dim(padded, core * half_boxes, half_boxes + 2 * HB, 0)
    window = jnp.transpose(window, (1, 0, 2))
    rows = lax.dynamic_slice_in_dim(near_box, core * half_boxes, half_boxes, 0)
    rows = rows - (device * boxes_here + core * half_boxes - HB)
    codes = lax.dynamic_slice_in_dim(near_code, core * half_boxes, half_boxes, 0)
    near = near_call(
        rows,
        codes,
        window[:, :, : 3 * half_pts],
        window[:, :, 3 * half_pts :].reshape(halves, half_boxes + 2 * HB, RHS, 2 * half_pts),
    )
    near = lax.all_gather(near, "dirs", axis=0, tiled=True)
    near = lax.dynamic_slice_in_dim(near, core * half_pts, half_pts, 2)
    near_real, near_imag = near[:, :RHS], near[:, RHS:]
    total_real = far_real + near_real
    total_imag = far_imag + near_imag
    return jnp.concatenate([total_real, total_imag], axis=-1).astype(jnp.bfloat16)[:, None]


def solution(mesh):
    return jax.shard_map(
        on_device,
        mesh=mesh,
        in_specs=(
            P("boxes", "dirs", None),
            P("boxes", "dirs", None, None),
            P("boxes", None),
            P("boxes", None),
            P("boxes", None),
            P("boxes", None),
            P("boxes", None),
            P("boxes", None),
            P("boxes", None),
            P("dirs", None, None),
            P("dirs", None, None),
            P(),
            P(),
        ),
        out_specs=P("boxes", "dirs", None, None),
        check_vma=False,
    )
```

```python
import functools
import math

import jax
import jax.numpy as jnp
import ml_dtypes
import numpy as np
from jax import lax
from jax.experimental import pallas as pl
from jax.experimental.pallas import tpu as pltpu
from jax.sharding import PartitionSpec as P

PTS = 128
EQ = 128
DIRS = 16
RHS = 4
NEAR = 27
CAP = 16
REACH = 2
HB = 8
PAR_DEV = 4
BOX_DEV = 32
HALF_BOX = 16
WINDOW = 64
FEATURES = 16

wave_number = 3.0
smoothing = 0.0625
sphere_radius = 2.5
golden_turn = 2.399963229728653
four_pi = 12.566370614359172

TURNS = wave_number / (2.0 * math.pi)
SCALE = TURNS * TURNS
COS_TERMS = (0.99995979, -19.73104169, 64.67343118, -82.40355071, 45.64655728)
SIN_TERMS = (6.2830558, -41.33121431, 81.36681533, -74.47800473, 32.78140114)
AMPLITUDE = TURNS / four_pi

F32, BF16 = jnp.float32, jnp.bfloat16


def surface_features():
    ordinal = np.arange(EQ).astype(np.float32)
    height = np.float32(1.0) - (np.float32(2.0) * ordinal + np.float32(1.0)) / np.float32(EQ)
    radial = np.sqrt(np.float32(1.0) - height * height)
    angles = ordinal * np.float32(golden_turn)
    surface = np.float32(sphere_radius) * np.stack(
        [radial * np.cos(angles), radial * np.sin(angles), height]
    )
    surface = surface.astype(np.float64)

    def split(values):
        parts = []
        for _ in range(3):
            part = values.astype(ml_dtypes.bfloat16).astype(np.float64)
            parts.append(part)
            values = values - part
        return parts

    coords = [split(-2.0 * SCALE * surface[k]) for k in range(3)]
    square = split(SCALE * ((surface * surface).sum(0) + smoothing))
    one = np.ones(EQ)
    rows = [coords[k][i] for i in range(3) for k in range(3)] + [one] * 3 + square + [0.0 * one]
    return np.stack(rows).astype(ml_dtypes.bfloat16)


def split3(values):
    high = values.astype(BF16).astype(F32)
    rest = values - high
    middle = rest.astype(BF16).astype(F32)
    return [high, middle, rest - middle]


def horner(terms, z):
    total = z * (AMPLITUDE * terms[-1]) + AMPLITUDE * terms[-2]
    for term in terms[-3::-1]:
        total = total * z + AMPLITUDE * term
    return total


def wave(scaled):
    inverse = lax.rsqrt(scaled)
    phase = scaled * inverse
    phase = phase - jnp.round(phase)
    z = phase * phase
    real = inverse * horner(COS_TERMS, z)
    imag = (inverse * phase) * horner(SIN_TERMS, z)
    return real.astype(BF16), imag.astype(BF16)


def source_features(coords):
    square = SCALE * sum(c * c for c in coords)
    one = jnp.ones_like(square)
    return coords * 3 + split3(square) + [one, one, one, jnp.zeros_like(one)]


def target_features(coords):
    square = SCALE * (sum(c * c for c in coords) + smoothing)
    one = jnp.ones_like(square)
    parts = [split3(-2.0 * SCALE * c) for c in coords]
    rows = [parts[k][i] for i in range(3) for k in range(3)]
    return rows + [one, one, one] + split3(square) + [jnp.zeros_like(one)]


def dot(a, b):
    return jnp.dot(a, b, preferred_element_type=F32)


def dot_nt(a, b):
    return lax.dot_general(a, b, (((1,), (1,)), ((), ())), preferred_element_type=F32)


def rows_at(start, step, size=None):
    return pl.ds(pl.multiple_of(start, step), size or step)


def one_hot(condition):
    return jnp.where(condition, 1.0, 0.0).astype(BF16)


def iota(shape, dim):
    return lax.broadcasted_iota(jnp.int32, shape, dim)


def kernel(
    grid,
    points_ref,
    charges_ref,
    near_box_ref,
    near_code_ref,
    send_ref,
    slot_ref,
    slot_dir_ref,
    coarse_ref,
    coarse_dir_ref,
    leaf_hbm,
    coarse_hbm,
    up_hbm,
    down_hbm,
    surf_x_ref,
    surf_y_ref,
    out_ref,
    pos_ref,
    own_ref,
    dense_ref,
    feature_ref,
    source_ref,
    target_ref,
    leaf_ref,
    coarse_tab_ref,
    up_ref,
    down_ref,
    hot_ref,
    hot_near_ref,
    raised_ref,
    outgoing_ref,
    send_buf,
    send_near,
    recv_buf,
    parent_buf,
    weight_ref,
    coarse_weight_ref,
    cone_ref,
    coarse_cone_ref,
    child_ref,
    local_ref,
    left_ref,
    near_ref,
    far_x_ref,
    far_ref,
    table_sem,
    pair_send,
    pair_recv,
    halo_send,
    halo_recv,
    all_send,
    all_recv,
    close_send,
    close_recv,
    parent_send,
    parent_recv,
):
    nz, nx, ny = grid
    peers = nz * nx * ny
    blocks = peers // 8
    me = lax.axis_index("boxes")
    core = lax.axis_index("dirs")
    other = 1 - core

    def around(step):
        return lax.rem(me + step + peers, peers)

    def remote(src, dst, send_sem, recv_sem, box_to, core_to):
        return pltpu.make_async_remote_copy(
            src_ref=src,
            dst_ref=dst,
            send_sem=send_sem,
            recv_sem=recv_sem,
            device_id=(box_to, core_to),
            device_id_type=pl.DeviceIdType.MESH,
        )

    points = points_ref[...].astype(F32)
    pos_ref[core, pl.ds(HB, BOX_DEV), :] = jnp.concatenate(
        [points, jnp.zeros((BOX_DEV, 64), F32)], axis=1
    )
    for k in range(3):
        piece = points[:, k * 64 : k * 64 + 64]
        own_ref[k] = jnp.concatenate([piece, piece], axis=1)
    sign = jnp.where(iota((RHS, 128), 1) < 64, 1.0, -1.0)

    def weigh(j, carry):
        q = charges_ref[j].astype(F32)
        both = jnp.concatenate([q * sign, pltpu.roll(q, 64, 1)], axis=0)
        dense_ref[core, HB + j] = jnp.concatenate(
            [both, jnp.zeros_like(both)], axis=0
        ).astype(BF16)
        return carry

    lax.fori_loop(0, BOX_DEV, weigh, 0, unroll=4)

    pair_copies = [
        remote(
            pos_ref.at[core, pl.ds(HB, BOX_DEV)],
            pos_ref.at[core, pl.ds(HB, BOX_DEV)],
            pair_send.at[0],
            pair_recv.at[0],
            me,
            other,
        ),
        remote(
            dense_ref.at[core, pl.ds(HB, BOX_DEV)],
            dense_ref.at[core, pl.ds(HB, BOX_DEV)],
            pair_send.at[1],
            pair_recv.at[1],
            me,
            other,
        ),
        remote(leaf_hbm, leaf_ref.at[core], pair_send.at[2], pair_recv.at[2], me, other),
        remote(coarse_hbm, coarse_tab_ref.at[core], pair_send.at[3], pair_recv.at[3], me, other),
    ]
    pair_copies[0].start()
    pair_copies[1].start()
    halo_copies = []
    edge = BOX_DEV + HB
    for side, (first, step) in enumerate(((BOX_DEV, 1), (HB, -1))):
        halo_copies.append(
            remote(
                pos_ref.at[core, pl.ds(first, HB)],
                pos_ref.at[core, pl.ds(side * edge, HB)],
                halo_send.at[2 * side],
                halo_recv.at[core],
                around(step),
                side,
            )
        )
        halo_copies.append(
            remote(
                dense_ref.at[core, pl.ds(first, HB)],
                dense_ref.at[core, pl.ds(side * edge, HB)],
                halo_send.at[2 * side + 1],
                halo_recv.at[2 + core],
                around(step),
                side,
            )
        )
    for copy in halo_copies:
        copy.start()
    table_copies = [
        pltpu.make_async_copy(up_hbm, up_ref, table_sem.at[0]),
        pltpu.make_async_copy(coarse_hbm, coarse_tab_ref.at[core], table_sem.at[1]),
        pltpu.make_async_copy(down_hbm, down_ref, table_sem.at[2]),
        pltpu.make_async_copy(leaf_hbm, leaf_ref.at[core], table_sem.at[3]),
    ]
    for copy in table_copies:
        copy.start()
    pair_copies[2].start()
    pair_copies[3].start()

    slot_row = iota((16, CAP), 0)
    slot_lane = iota((16, CAP), 1)
    first_slots = slot_lane == slot_row % 8
    last_slots = slot_lane == slot_row % 8 + 8
    column = iota((16, 64), 1).astype(F32) - (32 * (iota((16, 64), 0) // 8)).astype(F32)

    def slots_of(t, mask):
        row = send_ref[pl.ds(t, 1), :].astype(F32)
        wanted = jnp.sum(jnp.where(mask, row, 0.0), axis=1, keepdims=True)
        return one_hot(wanted == column)

    def mark(t, carry):
        hot_ref[rows_at(t * 16, 16), :] = slots_of(t, first_slots)
        return carry

    lax.fori_loop(0, peers, mark, 0, unroll=8)
    for index in range(5):
        hot_near_ref[pl.ds(index * 16, 16), :] = slots_of(around(index - REACH), last_slots)
    recv_buf[pl.ds((peers + 5) * 16, 48), :] = jnp.zeros((48, 256), BF16)

    def features(first, count):
        coords = [
            jnp.concatenate(
                [
                    pos_ref[0, rows_at(first, HB, count), :][:, k * 64 : k * 64 + 64],
                    pos_ref[1, rows_at(first, HB, count), :][:, k * 64 : k * 64 + 64],
                ],
                axis=1,
            )
            for k in range(3)
        ]
        for f, row in enumerate(source_features(coords)):
            feature_ref[pl.ds(first * FEATURES + f, count, stride=FEATURES), :] = row

        def turn(i, carry):
            j = first + i
            tile = feature_ref[rows_at(j * FEATURES, FEATURES), :]
            source_ref[j] = tile.T.astype(BF16)
            return carry

        lax.fori_loop(0, count, turn, 0, unroll=4)

    pair_copies[0].wait_recv()
    features(HB, BOX_DEV)
    pair_copies[1].wait_recv()

    def charges_at(j):
        return jnp.concatenate([dense_ref[0, j], dense_ref[1, j]], axis=1)

    def kernel_tile(y, x):
        parts = []
        for half in range(2):
            parts.extend(wave(dot(y[half * 64 : half * 64 + 64], x)))
        return jnp.concatenate(parts, axis=0)

    surf_x = surf_x_ref[...]

    def raise_box(b, carry):
        tile = kernel_tile(source_ref[HB + b], surf_x)
        raised_ref[rows_at(b * 8, 8), :] = dot(charges_at(HB + b), tile)[:8]
        return carry

    lax.fori_loop(0, BOX_DEV, raise_box, 0, unroll=4)
    outgoing = []
    for r in range(2):
        pieces = [
            raised_ref[pl.ds(2 * core + r + 4 * part, BOX_DEV, stride=8), :] for part in range(2)
        ]
        outgoing.append(jnp.concatenate(pieces, axis=1).astype(BF16))
    outgoing = jnp.concatenate(outgoing, axis=0)
    outgoing_ref[0] = outgoing[:, :128].astype(F32)
    outgoing_ref[1] = outgoing[:, 128:].astype(F32)

    def fill(block, carry):
        rows = rows_at(block * 128, 128)
        send_buf[rows, :] = dot(hot_ref[rows, :], outgoing).astype(BF16)
        return carry

    lax.fori_loop(0, blocks, fill, 0, unroll=min(4, blocks))
    send_near[...] = dot(hot_near_ref[...], outgoing).astype(BF16)

    def leaf_copy(t):
        return remote(
            send_buf.at[rows_at(t * 16, 16)],
            recv_buf.at[rows_at(me * 16, 16)],
            all_send,
            all_recv,
            t,
            core,
        )

    table_copies[0].wait()
    parent = jnp.zeros((8, 256), F32)
    for o in range(8):
        pieces = [outgoing_ref[part, pl.ds(o, 8, stride=8), :] for part in range(2)]
        parent += dot(jnp.concatenate(pieces, axis=1).astype(BF16), up_ref[o])
    mz, mx, my = me // (nx * ny), me // ny % nx, me % ny
    mine = (my * nx + mx) * nz + mz
    parent_buf[rows_at(mine * 16, 16), :] = jnp.concatenate(
        [parent[:, :128], parent[:, 128:]], axis=0
    ).astype(BF16)

    def parent_phase(phase):
        count = (nz, nx, ny)[phase]
        size = (16, 16 * nz, 16 * nz * nx)[phase]
        rows = rows_at((mine * 16) // size * size, size)
        copies = []
        for step in range(1, count):
            if phase == 0:
                to = lax.rem(mz + step, nz) * nx * ny + mx * ny + my
            elif phase == 1:
                to = mz * nx * ny + lax.rem(mx + step, nx) * ny + my
            else:
                to = mz * nx * ny + mx * ny + lax.rem(my + step, ny)
            copies.append(
                remote(
                    parent_buf.at[rows],
                    parent_buf.at[rows],
                    parent_send.at[phase],
                    parent_recv.at[phase],
                    to,
                    core,
                )
            )
        every = pl.ds(0, size * (count - 1))
        total = remote(
            parent_buf.at[every],
            parent_buf.at[every],
            parent_send.at[phase],
            parent_recv.at[phase],
            me,
            other,
        )
        return copies, total

    phases = [parent_phase(phase) for phase in range(3)]
    for copy in phases[0][0]:
        copy.start()

    def send_leaf(step, carry):
        leaf_copy(around(step)).start()
        return carry

    close_copies = []
    for index, step in enumerate((-2, -1, 1, 2)):
        close_copies.append(
            remote(
                send_near.at[pl.ds((step + REACH) * 16, 16)],
                recv_buf.at[pl.ds((peers + REACH - step) * 16, 16)],
                close_send.at[index],
                close_recv.at[index],
                around(step),
                core,
            )
        )
    for copy in close_copies:
        copy.start()
    lax.fori_loop(1, peers, send_leaf, 0)
    recv_buf[rows_at(me * 16, 16), :] = send_buf[rows_at(me * 16, 16), :]
    recv_buf[pl.ds((peers + REACH) * 16, 16), :] = send_near[pl.ds(REACH * 16, 16), :]

    for half in range(2):
        remote(
            pos_ref.at[half, pl.ds(HB, HB)],
            pos_ref.at[half, rows_at(core * edge, HB)],
            halo_send.at[0],
            halo_recv.at[half],
            me,
            other,
        ).wait_recv()
        remote(
            dense_ref.at[half, pl.ds(HB, HB)],
            dense_ref.at[half, pl.ds(core * edge, HB)],
            halo_send.at[1],
            halo_recv.at[2 + half],
            me,
            other,
        ).wait_recv()
    features(core * edge, HB)
    first_box = core * HALF_BOX
    near_rows = rows_at(HB + first_box, HB, HALF_BOX)
    mine_coords = [
        jnp.concatenate(
            [
                pos_ref[0, near_rows, :][:, k * 64 : k * 64 + 64],
                pos_ref[1, near_rows, :][:, k * 64 : k * 64 + 64],
            ],
            axis=1,
        )
        for k in range(3)
    ]
    for code in range(27):
        offset = (2.0 * (code // 9 - 1), 2.0 * (code // 3 % 3 - 1), 2.0 * (code % 3 - 1))
        moved = [c - o for c, o in zip(mine_coords, offset)]
        for f, row in enumerate(target_features(moved)):
            far_x_ref[pl.ds(f, HALF_BOX, stride=FEATURES), :] = row
        for b in range(HALF_BOX):
            target_ref[code * HALF_BOX + b] = far_x_ref[pl.ds(b * FEATURES, FEATURES), :].astype(
                BF16
            )

    def near_box_sum(b, carry):
        def group(g, total):
            for i in range(9):
                n = g * 9 + i
                j = (near_box_ref[first_box + b, n] - me * BOX_DEV + HB) & (WINDOW - 1)
                code = near_code_ref[first_box + b, n]
                tile = kernel_tile(source_ref[j], target_ref[code * HALF_BOX + b])
                total = total + dot(charges_at(j), tile)
            return total

        total = lax.fori_loop(0, 3, group, jnp.zeros((16, PTS), F32))
        near_ref[rows_at((first_box + b) * 8, 8), :] = total[:8]
        return carry

    lax.fori_loop(0, 5, near_box_sum, 0)
    phases[0][1].wait_recv()
    for copy in phases[1][0]:
        copy.start()
    lax.fori_loop(5, 10, near_box_sum, 0)
    phases[1][1].wait_recv()
    for copy in phases[2][0]:
        copy.start()
    lax.fori_loop(10, HALF_BOX, near_box_sum, 0)
    near_copy = remote(
        near_ref.at[rows_at(core * 128, 128)],
        near_ref.at[rows_at(core * 128, 128)],
        pair_send.at[4],
        pair_recv.at[4],
        me,
        other,
    )
    near_copy.start()

    lane = iota((HALF_BOX, 128), 1)
    pair_coords = [
        jnp.where(
            lane < 64,
            own_ref[k, pl.ds(0, HALF_BOX, stride=2), :],
            own_ref[k, pl.ds(1, HALF_BOX, stride=2), :],
        )
        for k in range(3)
    ]
    for f, row in enumerate(source_features(pair_coords)):
        far_x_ref[pl.ds(f, HALF_BOX, stride=FEATURES), :] = row
    surf_y = surf_y_ref[...]

    def lower(pair, carry):
        x = far_x_ref[rows_at(pair * FEATURES, FEATURES), :].astype(BF16)
        real, imag = wave(dot(surf_y, x))
        far_ref[rows_at(pair * 256, 256), :] = jnp.concatenate([real, imag], axis=0)
        return carry

    lax.fori_loop(0, HALF_BOX, lower, 0, unroll=2)

    head = iota(((blocks + 1) * 16, 128), 0)
    tail = iota((256, 128), 0)
    tail = tail % 128 - 8 * (tail // 128)

    def count_slots(b, carry):
        v = slot_ref[pl.ds(b, 1), :]
        s, c = v >> 4, v & 15
        late = c >= 8
        gap = (s - me + REACH) & (peers - 1)
        high = jnp.where(late, blocks, s >> 3)
        low = jnp.where(late, gap * 16 + c - 8, (s & 7) * 16 + c)
        a = one_hot(head == high * 16 + slot_dir_ref[pl.ds(b, 1), :])
        counts = dot_nt(a, one_hot(tail == low)).astype(BF16)
        for h in range(blocks + 1):
            for r in range(2):
                weight_ref[r, rows_at(b * 16, 16), pl.ds(h * 128, 128)] = counts[
                    h * 16 : h * 16 + 16, r * 128 : r * 128 + 128
                ]
        return carry

    lax.fori_loop(0, BOX_DEV, count_slots, 0)

    coarse_head = iota((blocks * 16, 32), 0)
    coarse_tail = iota((512, 32), 0)
    coarse_tail = coarse_tail % 128 - 4 * (coarse_tail // 128)
    for p in range(PAR_DEV):
        v = coarse_ref[pl.ds(p, 1), :]
        dev, q = v >> 2, v & 3
        dz, dx, dy = dev >> ((nx * ny).bit_length() - 1), dev >> (ny.bit_length() - 1), dev
        place = ((dy & (ny - 1)) * nx + (dx & (nx - 1))) * nz + dz
        a = one_hot(coarse_head == (place >> 3) * 16 + coarse_dir_ref[pl.ds(p, 1), :])
        counts = dot_nt(a, one_hot(coarse_tail == (place & 7) * 16 + q)).astype(BF16)
        for h in range(blocks):
            for part in range(4):
                coarse_weight_ref[part, pl.ds(p * 16, 16), pl.ds(h * 128, 128)] = counts[
                    h * 16 : h * 16 + 16, part * 128 : part * 128 + 128
                ]
    phases[2][1].wait_recv()
    parents = parent_buf[...]
    for part in range(4):
        coarse_cone_ref[part // 2, pl.ds(part % 2 * 64, 64), :] = dot(
            coarse_weight_ref[part], parents
        )
    table_copies[1].wait()
    pair_copies[3].wait_recv()
    coarse_local = jnp.zeros((8, 256), F32)
    for d in range(DIRS):
        pieces = [coarse_cone_ref[part, pl.ds(d, 8, stride=16), :] for part in range(2)]
        coarse_local += dot(
            jnp.concatenate(pieces, axis=1).astype(BF16), coarse_tab_ref[d // 8, d % 8]
        )
    coarse_local = coarse_local.astype(BF16)
    table_copies[2].wait()
    for o in range(8):
        child = dot(coarse_local, down_ref[o])
        for part in range(2):
            child_ref[part, pl.ds(o, 8, stride=8), :] = child[:, part * 128 : part * 128 + 128]

    every = pl.ds(0, (peers - 1) * 16)
    all_copies = remote(send_buf.at[every], recv_buf.at[every], all_send, all_recv, me, other)
    all_copies.wait_recv()
    for copy in close_copies:
        copy.wait_recv()

    def leaf_cones(block, carry):
        rows = rows_at(block * 128, 128)
        received = recv_buf[...]
        for r in range(2):
            cone = dot(weight_ref[r, rows, :], received)
            to = rows_at(r * 512 + block * 128, 128)
            cone_ref[0, to, :] = cone[:, :128]
            cone_ref[1, to, :] = cone[:, 128:]
        return carry

    lax.fori_loop(0, 4, leaf_cones, 0)
    table_copies[3].wait()
    pair_copies[2].wait_recv()
    local = jnp.concatenate([child_ref[0], child_ref[1]], axis=1)
    for d in range(DIRS):
        pieces = [cone_ref[part, pl.ds(d, 64, stride=16), :] for part in range(2)]
        local += dot(jnp.concatenate(pieces, axis=1).astype(BF16), leaf_ref[d // 8, d % 8])
    local_ref[core] = local.astype(BF16)
    local_copy = remote(
        local_ref.at[core], local_ref.at[core], pair_send.at[5], pair_recv.at[5], me, other
    )
    local_copy.start()
    near_copy.wait_recv()
    local_copy.wait_recv()
    for half in range(2):
        for r in range(2):
            piece = local_ref[half, pl.ds(r * BOX_DEV, BOX_DEV), :].astype(F32)
            real, imag = piece[:, :128], piece[:, 128:]
            row = 2 * half + r
            left_ref[0, pl.ds(row, BOX_DEV, stride=8), :] = real
            left_ref[1, pl.ds(row, BOX_DEV, stride=8), :] = -imag
            left_ref[0, pl.ds(row + RHS, BOX_DEV, stride=8), :] = imag
            left_ref[1, pl.ds(row + RHS, BOX_DEV, stride=8), :] = real
    lane = iota((16, 128), 1)
    swap = (iota((16, 128), 0) < 8) == (core == 1)
    low_lane = iota((RHS, 128), 1) < 64

    def finish(pair, carry):
        rows = rows_at(pair * 16, 16)
        left = jnp.concatenate([left_ref[0, rows, :], left_ref[1, rows, :]], axis=1).astype(BF16)
        near = near_ref[rows, :]
        total = dot(left, far_ref[rows_at(pair * 256, 256), :]) + jnp.where(
            swap, pltpu.roll(near, 64, 1), near
        )
        turned = pltpu.roll(total, 64, 1)
        out_ref[2 * pair, 0] = jnp.where(low_lane, total[0:4], turned[4:8]).astype(BF16)
        out_ref[2 * pair + 1, 0] = jnp.where(low_lane, turned[8:12], total[12:16]).astype(BF16)
        return carry

    lax.fori_loop(0, HALF_BOX, finish, 0, unroll=2)

    for copy in pair_copies + halo_copies + close_copies + [near_copy, local_copy]:
        copy.wait_send()
    all_copies.wait_send()
    for phase in range(3):
        phases[phase][1].wait_send()


def on_device(
    grid,
    points,
    charges,
    near_box,
    near_code,
    send_box,
    far_slot,
    far_direction,
    coarse_source,
    coarse_direction,
    leaf_translate,
    coarse_translate,
    child_to_parent,
    parent_to_child,
):
    peers = grid[0] * grid[1] * grid[2]
    blocks = peers // 8
    vmem = pl.BlockSpec(memory_space=pltpu.VMEM)
    smem = pl.BlockSpec(memory_space=pltpu.SMEM)
    hbm = pl.BlockSpec(memory_space=pl.ANY)
    surf = surface_features()
    dma = pltpu.SemaphoreType.DMA
    return pl.pallas_call(
        functools.partial(kernel, grid),
        out_shape=jax.ShapeDtypeStruct((BOX_DEV, 1, RHS, 128), BF16),
        in_specs=[vmem, vmem, smem, smem, vmem, vmem, vmem, vmem, vmem]
        + [hbm, hbm, hbm, hbm, vmem, vmem],
        out_specs=vmem,
        scratch_shapes=[
            pltpu.VMEM((2, WINDOW, 256), F32),
            pltpu.VMEM((3, BOX_DEV, 128), F32),
            pltpu.VMEM((2, WINDOW, 16, 128), BF16),
            pltpu.VMEM((WINDOW * FEATURES, 128), F32),
            pltpu.VMEM((WINDOW, PTS, FEATURES), BF16),
            pltpu.VMEM((27 * HALF_BOX, FEATURES, 128), BF16),
            pltpu.VMEM((2, 8, 256, 256), BF16),
            pltpu.VMEM((2, 8, 256, 256), BF16),
            pltpu.VMEM((8, 256, 256), BF16),
            pltpu.VMEM((8, 256, 256), BF16),
            pltpu.VMEM((peers * 16, 64), BF16),
            pltpu.VMEM((5 * 16, 64), BF16),
            pltpu.VMEM((BOX_DEV * 8, 128), F32),
            pltpu.VMEM((2, 64, 128), F32),
            pltpu.VMEM((peers * 16, 256), BF16),
            pltpu.VMEM((5 * 16, 256), BF16),
            pltpu.VMEM(((peers + 8) * 16, 256), BF16),
            pltpu.VMEM((peers * 16, 128), BF16),
            pltpu.VMEM((2, BOX_DEV * DIRS, (blocks + 1) * 128), BF16),
            pltpu.VMEM((4, PAR_DEV * DIRS, blocks * 128), BF16),
            pltpu.VMEM((2, 2 * BOX_DEV * DIRS, 128), F32),
            pltpu.VMEM((2, 2 * PAR_DEV * DIRS, 128), F32),
            pltpu.VMEM((2, 64, 128), F32),
            pltpu.VMEM((2, 64, 256), BF16),
            pltpu.VMEM((2, BOX_DEV * 8, 128), F32),
            pltpu.VMEM((BOX_DEV * 8, 128), F32),
            pltpu.VMEM((HALF_BOX * FEATURES, 128), F32),
            pltpu.VMEM((HALF_BOX * 256, 128), BF16),
            dma((4,)),
            dma((6,)),
            dma((6,)),
            dma((4,)),
            dma((4,)),
            dma,
            dma,
            dma((4,)),
            dma((4,)),
            dma((3,)),
            dma((3,)),
        ],
        compiler_params=pltpu.CompilerParams(
            has_side_effects=True, vmem_limit_bytes=48 * 1024 * 1024
        ),
        cost_estimate=pl.CostEstimate(
            flops=5 * 10**9, bytes_accessed=10**7, transcendentals=10**7
        ),
        name="multipole",
    )(
        points[:, 0],
        charges[:, 0],
        near_box,
        near_code,
        send_box,
        far_slot,
        far_direction,
        coarse_source,
        coarse_direction,
        leaf_translate,
        coarse_translate,
        child_to_parent,
        parent_to_child,
        jnp.asarray(surf),
        jnp.asarray(np.ascontiguousarray(surf.T)),
    )


def solution(mesh):
    peers = mesh.shape["boxes"]
    grid = {128: (8, 4, 4), 8: (2, 2, 2)}[peers]
    return jax.shard_map(
        functools.partial(on_device, grid),
        mesh=mesh,
        in_specs=(
            P("boxes", "dirs", None),
            P("boxes", "dirs", None, None),
            P("boxes", None),
            P("boxes", None),
            P("boxes", None),
            P("boxes", None),
            P("boxes", None),
            P("boxes", None),
            P("boxes", None),
            P("dirs", None, None),
            P("dirs", None, None),
            P(),
            P(),
        ),
        out_specs=P("boxes", "dirs", None, None),
        check_vma=False,
    )
```

```python
import functools
import math

import jax
import jax.numpy as jnp
import ml_dtypes
import numpy as np
from jax import lax
from jax.experimental import pallas as pl
from jax.experimental.pallas import tpu as pltpu
from jax.sharding import PartitionSpec as P

PTS = 128
EQ = 128
DIRS = 16
RHS = 4
NEAR = 27
CAP = 16
REACH = 2
HB = 8
PAR_DEV = 4
BOX_DEV = 32
HALF_BOX = 16
WINDOW = 64
FEATURES = 16

wave_number = 3.0
smoothing = 0.0625
sphere_radius = 2.5
golden_turn = 2.399963229728653
four_pi = 12.566370614359172

TURNS = wave_number / (2.0 * math.pi)
SCALE = TURNS * TURNS
COS_TERMS = (0.99995979, -19.73104169, 64.67343118, -82.40355071, 45.64655728)
SIN_TERMS = (6.2830558, -41.33121431, 81.36681533, -74.47800473, 32.78140114)
AMPLITUDE = TURNS / four_pi

VMEM_BYTES = 62 * 1024 * 1024
F32, BF16 = jnp.float32, jnp.bfloat16


def surface_features():
    ordinal = np.arange(EQ).astype(np.float32)
    height = np.float32(1.0) - (np.float32(2.0) * ordinal + np.float32(1.0)) / np.float32(EQ)
    radial = np.sqrt(np.float32(1.0) - height * height)
    angles = ordinal * np.float32(golden_turn)
    surface = np.float32(sphere_radius) * np.stack(
        [radial * np.cos(angles), radial * np.sin(angles), height]
    )
    surface = surface.astype(np.float64)

    def split(values):
        parts = []
        for _ in range(3):
            part = values.astype(ml_dtypes.bfloat16).astype(np.float64)
            parts.append(part)
            values = values - part
        return parts

    coords = [split(-2.0 * SCALE * surface[k]) for k in range(3)]
    square = split(SCALE * ((surface * surface).sum(0) + smoothing))
    one = np.ones(EQ)
    rows = [coords[k][i] for i in range(3) for k in range(3)] + [one] * 3 + square + [0.0 * one]
    return np.stack(rows).astype(ml_dtypes.bfloat16)


def split3(values):
    high = values.astype(BF16).astype(F32)
    rest = values - high
    middle = rest.astype(BF16).astype(F32)
    return [high, middle, rest - middle]


def horner(terms, z):
    total = z * (AMPLITUDE * terms[-1]) + AMPLITUDE * terms[-2]
    for term in terms[-3::-1]:
        total = total * z + AMPLITUDE * term
    return total


def wave(scaled):
    inverse = lax.rsqrt(scaled)
    phase = scaled * inverse
    phase = phase - jnp.round(phase)
    z = phase * phase
    real = inverse * horner(COS_TERMS, z)
    imag = (inverse * phase) * horner(SIN_TERMS, z)
    return real.astype(BF16), imag.astype(BF16)


def source_features(coords):
    square = SCALE * sum(c * c for c in coords)
    one = jnp.ones_like(square)
    return coords * 3 + split3(square) + [one, one, one, jnp.zeros_like(one)]


def target_features(coords):
    square = SCALE * (sum(c * c for c in coords) + smoothing)
    one = jnp.ones_like(square)
    parts = [split3(-2.0 * SCALE * c) for c in coords]
    rows = [parts[k][i] for i in range(3) for k in range(3)]
    return rows + [one, one, one] + split3(square) + [jnp.zeros_like(one)]


def dot(a, b):
    return jnp.dot(a, b, preferred_element_type=F32)


def dot_nt(a, b):
    return lax.dot_general(a, b, (((1,), (1,)), ((), ())), preferred_element_type=F32)


def rows_at(start, step, size=None):
    return pl.ds(pl.multiple_of(start, step), size or step)


def one_hot(condition):
    return jnp.where(condition, 1.0, 0.0).astype(BF16)


def iota(shape, dim):
    return lax.broadcasted_iota(jnp.int32, shape, dim)


def kernel(
    grid,
    points_ref,
    charges_ref,
    near_box_ref,
    near_code_ref,
    send_hbm,
    slot_hbm,
    slot_dir_hbm,
    coarse_source_hbm,
    coarse_dir_hbm,
    leaf_hbm,
    coarse_hbm,
    up_hbm,
    down_hbm,
    surf_x_ref,
    surf_y_ref,
    out_ref,
    pos_ref,
    own_ref,
    dense_ref,
    feature_ref,
    source_ref,
    target_ref,
    leaf_ref,
    coarse_tab_ref,
    up_ref,
    down_ref,
    hot_ref,
    hot_near_ref,
    raised_ref,
    outgoing_ref,
    send_buf,
    send_near,
    recv_buf,
    parent_buf,
    weight_ref,
    coarse_weight_ref,
    cone_ref,
    coarse_cone_ref,
    child_ref,
    local_ref,
    left_ref,
    near_ref,
    far_x_ref,
    far_ref,
    send_ref,
    slot_ref,
    slot_dir_ref,
    coarse_ref,
    coarse_dir_ref,
    table_sem,
    list_sem,
    pair_send,
    pair_recv,
    halo_send,
    halo_recv,
    all_send,
    all_recv,
    close_send,
    close_recv,
    parent_send,
    parent_recv,
):
    nz, nx, ny = grid
    peers = nz * nx * ny
    blocks = peers // 8
    me = lax.axis_index("boxes")
    core = lax.axis_index("dirs")
    other = 1 - core

    def around(step):
        return lax.rem(me + step + peers, peers)

    def remote(src, dst, send_sem, recv_sem, box_to, core_to):
        return pltpu.make_async_remote_copy(
            src_ref=src,
            dst_ref=dst,
            send_sem=send_sem,
            recv_sem=recv_sem,
            device_id=(box_to, core_to),
            device_id_type=pl.DeviceIdType.MESH,
        )

    list_copies = [
        pltpu.make_async_copy(src, dst, list_sem.at[i])
        for i, (src, dst) in enumerate(
            (
                (send_hbm, send_ref),
                (slot_hbm, slot_ref),
                (slot_dir_hbm, slot_dir_ref),
                (coarse_source_hbm, coarse_ref),
                (coarse_dir_hbm, coarse_dir_ref),
            )
        )
    ]
    for copy in list_copies:
        copy.start()

    points = points_ref[...].astype(F32)
    pos_ref[core, pl.ds(HB, BOX_DEV), :] = jnp.concatenate(
        [points, jnp.zeros((BOX_DEV, 64), F32)], axis=1
    )
    for k in range(3):
        piece = points[:, k * 64 : k * 64 + 64]
        own_ref[k] = jnp.concatenate([piece, piece], axis=1)
    sign = jnp.where(iota((RHS, 128), 1) < 64, 1.0, -1.0)

    def weigh(j, carry):
        q = charges_ref[j].astype(F32)
        both = jnp.concatenate([q * sign, pltpu.roll(q, 64, 1)], axis=0)
        dense_ref[core, HB + j] = jnp.concatenate([both, both], axis=0).astype(BF16)
        return carry

    lax.fori_loop(0, BOX_DEV, weigh, 0, unroll=4)

    pair_copies = [
        remote(
            pos_ref.at[core, pl.ds(HB, BOX_DEV)],
            pos_ref.at[core, pl.ds(HB, BOX_DEV)],
            pair_send.at[0],
            pair_recv.at[0],
            me,
            other,
        ),
        remote(
            dense_ref.at[core, pl.ds(HB, BOX_DEV)],
            dense_ref.at[core, pl.ds(HB, BOX_DEV)],
            pair_send.at[1],
            pair_recv.at[1],
            me,
            other,
        ),
        remote(leaf_hbm, leaf_ref.at[core], pair_send.at[2], pair_recv.at[2], me, other),
        remote(coarse_hbm, coarse_tab_ref.at[core], pair_send.at[3], pair_recv.at[3], me, other),
    ]
    pair_copies[0].start()
    pair_copies[1].start()
    halo_copies = []
    edge = BOX_DEV + HB
    for side, (first, step) in enumerate(((BOX_DEV, 1), (HB, -1))):
        halo_copies.append(
            remote(
                pos_ref.at[core, pl.ds(first, HB)],
                pos_ref.at[core, pl.ds(side * edge, HB)],
                halo_send.at[2 * side],
                halo_recv.at[core],
                around(step),
                side,
            )
        )
        halo_copies.append(
            remote(
                dense_ref.at[core, pl.ds(first, HB)],
                dense_ref.at[core, pl.ds(side * edge, HB)],
                halo_send.at[2 * side + 1],
                halo_recv.at[2 + core],
                around(step),
                side,
            )
        )
    for copy in halo_copies:
        copy.start()
    table_copies = [
        pltpu.make_async_copy(up_hbm, up_ref, table_sem.at[0]),
        pltpu.make_async_copy(coarse_hbm, coarse_tab_ref.at[core], table_sem.at[1]),
        pltpu.make_async_copy(down_hbm, down_ref, table_sem.at[2]),
        pltpu.make_async_copy(leaf_hbm, leaf_ref.at[core], table_sem.at[3]),
    ]
    for copy in table_copies:
        copy.start()
    pair_copies[2].start()
    pair_copies[3].start()

    list_copies[0].wait()
    slot_row = iota((16, CAP), 0)
    slot_lane = iota((16, CAP), 1)
    first_slots = slot_lane == slot_row % 8
    last_slots = slot_lane == slot_row % 8 + 8
    column = iota((16, 64), 1).astype(F32) - (32 * (iota((16, 64), 0) // 8)).astype(F32)

    def slots_of(t, mask):
        row = send_ref[pl.ds(t, 1), :].astype(F32)
        wanted = jnp.sum(jnp.where(mask, row, 0.0), axis=1, keepdims=True)
        return one_hot(wanted == column)

    def mark(t, carry):
        hot_ref[rows_at(t * 16, 16), :] = slots_of(t, first_slots)
        return carry

    lax.fori_loop(0, peers, mark, 0, unroll=8)
    for index in range(5):
        hot_near_ref[pl.ds(index * 16, 16), :] = slots_of(around(index - REACH), last_slots)
    recv_buf[pl.ds((peers + 5) * 16, 48), :] = jnp.zeros((48, 256), BF16)

    def features(first, count):
        coords = [
            jnp.concatenate(
                [
                    pos_ref[0, rows_at(first, HB, count), :][:, k * 64 : k * 64 + 64],
                    pos_ref[1, rows_at(first, HB, count), :][:, k * 64 : k * 64 + 64],
                ],
                axis=1,
            )
            for k in range(3)
        ]
        for f, row in enumerate(source_features(coords)):
            feature_ref[pl.ds(first * FEATURES + f, count, stride=FEATURES), :] = row

        def turn(i, carry):
            j = first + i
            tile = feature_ref[rows_at(j * FEATURES, FEATURES), :]
            turned = tile.T
            blank = jnp.zeros_like(turned)
            source_ref[0, j] = jnp.concatenate([turned, blank], axis=1).astype(BF16)
            source_ref[1, j] = jnp.concatenate([blank, turned], axis=1).astype(BF16)
            return carry

        lax.fori_loop(0, count, turn, 0, unroll=4)

    pair_copies[0].wait_recv()
    features(HB, BOX_DEV)
    pair_copies[1].wait_recv()

    def charges_at(j):
        return jnp.concatenate([dense_ref[0, j], dense_ref[1, j]], axis=1)

    def kernel_tile(y, x):
        parts = []
        for half in range(2):
            pieces = [wave(dot(y[at : at + 32], x)) for at in (half * 64, half * 64 + 32)]
            parts.extend([piece[0] for piece in pieces] + [piece[1] for piece in pieces])
        return jnp.concatenate(parts, axis=0)

    surf_x = surf_x_ref[...]

    def raise_box(b, carry):
        tile = kernel_tile(source_ref[0, HB + b][:, :FEATURES], surf_x)
        raised_ref[rows_at(b * 8, 8), :] = dot(charges_at(HB + b), tile)[:8]
        return carry

    lax.fori_loop(0, BOX_DEV, raise_box, 0, unroll=4)
    outgoing = []
    for r in range(2):
        pieces = [
            raised_ref[pl.ds(2 * core + r + 4 * part, BOX_DEV, stride=8), :] for part in range(2)
        ]
        outgoing.append(jnp.concatenate(pieces, axis=1).astype(BF16))
    outgoing = jnp.concatenate(outgoing, axis=0)
    outgoing_ref[0] = outgoing[:, :128].astype(F32)
    outgoing_ref[1] = outgoing[:, 128:].astype(F32)

    def fill(block, carry):
        rows = rows_at(block * 128, 128)
        send_buf[rows, :] = dot(hot_ref[rows, :], outgoing).astype(BF16)
        return carry

    lax.fori_loop(0, blocks, fill, 0, unroll=min(4, blocks))
    send_near[...] = dot(hot_near_ref[...], outgoing).astype(BF16)

    def leaf_copy(t):
        return remote(
            send_buf.at[rows_at(t * 16, 16)],
            recv_buf.at[rows_at(me * 16, 16)],
            all_send,
            all_recv,
            t,
            core,
        )

    table_copies[0].wait()
    parent = jnp.zeros((8, 256), F32)
    for o in range(8):
        pieces = [outgoing_ref[part, pl.ds(o, 8, stride=8), :] for part in range(2)]
        parent += dot(jnp.concatenate(pieces, axis=1).astype(BF16), up_ref[o])
    mz, mx, my = me // (nx * ny), me // ny % nx, me % ny
    mine = (my * nx + mx) * nz + mz
    parent_buf[rows_at(mine * 16, 16), :] = jnp.concatenate(
        [parent[:, :128], parent[:, 128:]], axis=0
    ).astype(BF16)

    def parent_phase(phase):
        count = (nz, nx, ny)[phase]
        size = (16, 16 * nz, 16 * nz * nx)[phase]
        rows = rows_at((mine * 16) // size * size, size)
        copies = []
        for step in range(1, count):
            if phase == 0:
                to = lax.rem(mz + step, nz) * nx * ny + mx * ny + my
            elif phase == 1:
                to = mz * nx * ny + lax.rem(mx + step, nx) * ny + my
            else:
                to = mz * nx * ny + mx * ny + lax.rem(my + step, ny)
            copies.append(
                remote(
                    parent_buf.at[rows],
                    parent_buf.at[rows],
                    parent_send.at[phase],
                    parent_recv.at[phase],
                    to,
                    core,
                )
            )
        every = pl.ds(0, size * (count - 1))
        total = remote(
            parent_buf.at[every],
            parent_buf.at[every],
            parent_send.at[phase],
            parent_recv.at[phase],
            me,
            other,
        )
        return copies, total

    phases = [parent_phase(phase) for phase in range(3)]
    for copy in phases[0][0]:
        copy.start()

    def send_leaf(step, carry):
        leaf_copy(around(step)).start()
        return carry

    close_copies = []
    for index, step in enumerate((-2, -1, 1, 2)):
        close_copies.append(
            remote(
                send_near.at[pl.ds((step + REACH) * 16, 16)],
                recv_buf.at[pl.ds((peers + REACH - step) * 16, 16)],
                close_send.at[index],
                close_recv.at[index],
                around(step),
                core,
            )
        )
    for copy in close_copies:
        copy.start()
    lax.fori_loop(1, peers, send_leaf, 0)
    recv_buf[rows_at(me * 16, 16), :] = send_buf[rows_at(me * 16, 16), :]
    recv_buf[pl.ds((peers + REACH) * 16, 16), :] = send_near[pl.ds(REACH * 16, 16), :]

    for half in range(2):
        remote(
            pos_ref.at[half, pl.ds(HB, HB)],
            pos_ref.at[half, rows_at(core * edge, HB)],
            halo_send.at[0],
            halo_recv.at[half],
            me,
            other,
        ).wait_recv()
        remote(
            dense_ref.at[half, pl.ds(HB, HB)],
            dense_ref.at[half, pl.ds(core * edge, HB)],
            halo_send.at[1],
            halo_recv.at[2 + half],
            me,
            other,
        ).wait_recv()
    features(core * edge, HB)
    first_box = core * HALF_BOX
    near_rows = rows_at(HB + first_box, HB, HALF_BOX)
    mine_coords = [
        jnp.concatenate(
            [
                pos_ref[0, near_rows, :][:, k * 64 : k * 64 + 64],
                pos_ref[1, near_rows, :][:, k * 64 : k * 64 + 64],
            ],
            axis=1,
        )
        for k in range(3)
    ]
    for code in range(27):
        offset = (2.0 * (code // 9 - 1), 2.0 * (code // 3 % 3 - 1), 2.0 * (code % 3 - 1))
        moved = [c - o for c, o in zip(mine_coords, offset)]
        for f, row in enumerate(target_features(moved)):
            far_x_ref[pl.ds(f, HALF_BOX, stride=FEATURES), :] = row
        for b in range(HALF_BOX):
            target_ref[code * HALF_BOX + b] = far_x_ref[pl.ds(b * FEATURES, FEATURES), :].astype(
                BF16
            )

    upper = iota((16, 256), 0) < 8
    pad = jnp.zeros((FEATURES, PTS), BF16)

    def near_pair_sum(pair, carry):
        b = 2 * pair

        def group(g, total):
            for i in range(9):
                n = g * 9 + i
                j, code = [], []
                for k in range(2):
                    place = near_box_ref[first_box + b + k, n] - me * BOX_DEV + HB
                    j.append(place & (WINDOW - 1))
                    code.append(near_code_ref[first_box + b + k, n] * HALF_BOX + b + k)
                y = source_ref[0, j[0]] + source_ref[1, j[1]]
                x = jnp.concatenate(
                    [
                        jnp.concatenate([target_ref[code[0]], pad], axis=1),
                        jnp.concatenate([pad, target_ref[code[1]]], axis=1),
                    ],
                    axis=0,
                )
                q = jnp.where(upper, charges_at(j[0]), charges_at(j[1]))
                total = total + dot(q, kernel_tile(y, x))
            return total

        total = lax.fori_loop(0, 3, group, jnp.zeros((16, 2 * PTS), F32))
        near_ref[rows_at((first_box + b) * 8, 16), :] = jnp.concatenate(
            [total[:8, :PTS], total[8:, PTS:]], axis=0
        )
        return carry

    lax.fori_loop(0, 2, near_pair_sum, 0)
    phases[0][1].wait_recv()
    for copy in phases[1][0]:
        copy.start()
    lax.fori_loop(2, 5, near_pair_sum, 0)
    phases[1][1].wait_recv()
    for copy in phases[2][0]:
        copy.start()
    lax.fori_loop(5, HALF_BOX // 2, near_pair_sum, 0)
    near_copy = remote(
        near_ref.at[rows_at(core * 128, 128)],
        near_ref.at[rows_at(core * 128, 128)],
        pair_send.at[4],
        pair_recv.at[4],
        me,
        other,
    )
    near_copy.start()

    lane = iota((HALF_BOX, 128), 1)
    pair_coords = [
        jnp.where(
            lane < 64,
            own_ref[k, pl.ds(0, HALF_BOX, stride=2), :],
            own_ref[k, pl.ds(1, HALF_BOX, stride=2), :],
        )
        for k in range(3)
    ]
    for f, row in enumerate(source_features(pair_coords)):
        far_x_ref[pl.ds(f, HALF_BOX, stride=FEATURES), :] = row
    surf_y = surf_y_ref[...]

    def lower(pair, carry):
        x = far_x_ref[rows_at(pair * FEATURES, FEATURES), :].astype(BF16)
        real, imag = wave(dot(surf_y, x))
        far_ref[rows_at(pair * 256, 256), :] = jnp.concatenate([real, imag], axis=0)
        return carry

    lax.fori_loop(0, HALF_BOX, lower, 0, unroll=2)

    for copy in list_copies[1:]:
        copy.wait()
    head = iota(((blocks + 1) * 16, 128), 0)
    tail = iota((256, 128), 0)
    tail = tail % 128 - 8 * (tail // 128)

    def count_slots(b, carry):
        v = slot_ref[pl.ds(b, 1), :]
        s, c = v >> 4, v & 15
        late = c >= 8
        gap = (s - me + REACH) & (peers - 1)
        high = jnp.where(late, blocks, s >> 3)
        low = jnp.where(late, gap * 16 + c - 8, (s & 7) * 16 + c)
        a = one_hot(head == high * 16 + slot_dir_ref[pl.ds(b, 1), :])
        counts = dot_nt(a, one_hot(tail == low)).astype(BF16)
        for h in range(blocks + 1):
            for r in range(2):
                weight_ref[r, rows_at(b * 16, 16), pl.ds(h * 128, 128)] = counts[
                    h * 16 : h * 16 + 16, r * 128 : r * 128 + 128
                ]
        return carry

    lax.fori_loop(0, BOX_DEV, count_slots, 0)

    coarse_head = iota((blocks * 16, 32), 0)
    coarse_tail = iota((512, 32), 0)
    coarse_tail = coarse_tail % 128 - 4 * (coarse_tail // 128)
    for p in range(PAR_DEV):
        v = coarse_ref[pl.ds(p, 1), :]
        dev, q = v >> 2, v & 3
        dz, dx, dy = dev >> ((nx * ny).bit_length() - 1), dev >> (ny.bit_length() - 1), dev
        place = ((dy & (ny - 1)) * nx + (dx & (nx - 1))) * nz + dz
        a = one_hot(coarse_head == (place >> 3) * 16 + coarse_dir_ref[pl.ds(p, 1), :])
        counts = dot_nt(a, one_hot(coarse_tail == (place & 7) * 16 + q)).astype(BF16)
        for h in range(blocks):
            for part in range(4):
                coarse_weight_ref[part, pl.ds(p * 16, 16), pl.ds(h * 128, 128)] = counts[
                    h * 16 : h * 16 + 16, part * 128 : part * 128 + 128
                ]
    phases[2][1].wait_recv()
    parents = parent_buf[...]
    for part in range(4):
        coarse_cone_ref[part // 2, pl.ds(part % 2 * 64, 64), :] = dot(
            coarse_weight_ref[part], parents
        )
    table_copies[1].wait()
    pair_copies[3].wait_recv()
    coarse_local = jnp.zeros((8, 256), F32)
    for d in range(DIRS):
        pieces = [coarse_cone_ref[part, pl.ds(d, 8, stride=16), :] for part in range(2)]
        coarse_local += dot(
            jnp.concatenate(pieces, axis=1).astype(BF16), coarse_tab_ref[d // 8, d % 8]
        )
    coarse_local = coarse_local.astype(BF16)
    table_copies[2].wait()
    for o in range(8):
        child = dot(coarse_local, down_ref[o])
        for part in range(2):
            child_ref[part, pl.ds(o, 8, stride=8), :] = child[:, part * 128 : part * 128 + 128]

    every = pl.ds(0, (peers - 1) * 16)
    all_copies = remote(send_buf.at[every], recv_buf.at[every], all_send, all_recv, me, other)
    all_copies.wait_recv()
    for copy in close_copies:
        copy.wait_recv()

    def leaf_cones(block, carry):
        rows = rows_at(block * 128, 128)
        received = recv_buf[...]
        for r in range(2):
            cone = dot(weight_ref[r, rows, :], received)
            to = rows_at(r * 512 + block * 128, 128)
            cone_ref[0, to, :] = cone[:, :128]
            cone_ref[1, to, :] = cone[:, 128:]
        return carry

    lax.fori_loop(0, 4, leaf_cones, 0)
    table_copies[3].wait()
    pair_copies[2].wait_recv()
    local = jnp.concatenate([child_ref[0], child_ref[1]], axis=1)
    for d in range(DIRS):
        pieces = [cone_ref[part, pl.ds(d, 64, stride=16), :] for part in range(2)]
        local += dot(jnp.concatenate(pieces, axis=1).astype(BF16), leaf_ref[d // 8, d % 8])
    local_ref[core] = local.astype(BF16)
    local_copy = remote(
        local_ref.at[core], local_ref.at[core], pair_send.at[5], pair_recv.at[5], me, other
    )
    local_copy.start()
    near_copy.wait_recv()
    local_copy.wait_recv()
    for half in range(2):
        for r in range(2):
            piece = local_ref[half, pl.ds(r * BOX_DEV, BOX_DEV), :].astype(F32)
            real, imag = piece[:, :128], piece[:, 128:]
            row = 2 * half + r
            left_ref[0, pl.ds(row, BOX_DEV, stride=8), :] = real
            left_ref[1, pl.ds(row, BOX_DEV, stride=8), :] = -imag
            left_ref[0, pl.ds(row + RHS, BOX_DEV, stride=8), :] = imag
            left_ref[1, pl.ds(row + RHS, BOX_DEV, stride=8), :] = real
    lane = iota((16, 128), 1)
    swap = (iota((16, 128), 0) < 8) == (core == 1)
    low_lane = iota((RHS, 128), 1) < 64

    def finish(pair, carry):
        rows = rows_at(pair * 16, 16)
        left = jnp.concatenate([left_ref[0, rows, :], left_ref[1, rows, :]], axis=1).astype(BF16)
        near = near_ref[rows, :]
        total = dot(left, far_ref[rows_at(pair * 256, 256), :]) + jnp.where(
            swap, pltpu.roll(near, 64, 1), near
        )
        turned = pltpu.roll(total, 64, 1)
        out_ref[2 * pair, 0] = jnp.where(low_lane, total[0:4], turned[4:8]).astype(BF16)
        out_ref[2 * pair + 1, 0] = jnp.where(low_lane, turned[8:12], total[12:16]).astype(BF16)
        return carry

    lax.fori_loop(0, HALF_BOX, finish, 0, unroll=2)

    for copy in pair_copies + halo_copies + close_copies + [near_copy, local_copy]:
        copy.wait_send()
    all_copies.wait_send()
    for phase in range(3):
        phases[phase][1].wait_send()


def on_device(
    grid,
    points,
    charges,
    near_box,
    near_code,
    send_box,
    far_slot,
    far_direction,
    coarse_source,
    coarse_direction,
    leaf_translate,
    coarse_translate,
    child_to_parent,
    parent_to_child,
):
    peers = grid[0] * grid[1] * grid[2]
    blocks = peers // 8
    vmem = pl.BlockSpec(memory_space=pltpu.VMEM)
    smem = pl.BlockSpec(memory_space=pltpu.SMEM)
    hbm = pl.BlockSpec(memory_space=pl.ANY)
    surf = surface_features()
    dma = pltpu.SemaphoreType.DMA
    return pl.pallas_call(
        functools.partial(kernel, grid),
        out_shape=jax.ShapeDtypeStruct((BOX_DEV, 1, RHS, 128), BF16),
        in_specs=[vmem, vmem, smem, smem] + [hbm] * 9 + [vmem, vmem],
        out_specs=vmem,
        scratch_shapes=[
            pltpu.VMEM((2, WINDOW, 256), F32),
            pltpu.VMEM((3, BOX_DEV, 128), F32),
            pltpu.VMEM((2, WINDOW, 16, 128), BF16),
            pltpu.VMEM((WINDOW * FEATURES, 128), F32),
            pltpu.VMEM((2, WINDOW, PTS, 2 * FEATURES), BF16),
            pltpu.VMEM((27 * HALF_BOX, FEATURES, 128), BF16),
            pltpu.VMEM((2, 8, 256, 256), BF16),
            pltpu.VMEM((2, 8, 256, 256), BF16),
            pltpu.VMEM((8, 256, 256), BF16),
            pltpu.VMEM((8, 256, 256), BF16),
            pltpu.VMEM((peers * 16, 64), BF16),
            pltpu.VMEM((5 * 16, 64), BF16),
            pltpu.VMEM((BOX_DEV * 8, 128), F32),
            pltpu.VMEM((2, 64, 128), F32),
            pltpu.VMEM((peers * 16, 256), BF16),
            pltpu.VMEM((5 * 16, 256), BF16),
            pltpu.VMEM(((peers + 8) * 16, 256), BF16),
            pltpu.VMEM((peers * 16, 128), BF16),
            pltpu.VMEM((2, BOX_DEV * DIRS, (blocks + 1) * 128), BF16),
            pltpu.VMEM((4, PAR_DEV * DIRS, blocks * 128), BF16),
            pltpu.VMEM((2, 2 * BOX_DEV * DIRS, 128), F32),
            pltpu.VMEM((2, 2 * PAR_DEV * DIRS, 128), F32),
            pltpu.VMEM((2, 64, 128), F32),
            pltpu.VMEM((2, 64, 256), BF16),
            pltpu.VMEM((2, BOX_DEV * 8, 128), F32),
            pltpu.VMEM((BOX_DEV * 8, 128), F32),
            pltpu.VMEM((HALF_BOX * FEATURES, 128), F32),
            pltpu.VMEM((HALF_BOX * 256, 128), BF16),
            pltpu.VMEM((peers, CAP), jnp.int32),
            pltpu.VMEM((BOX_DEV, 128), jnp.int32),
            pltpu.VMEM((BOX_DEV, 128), jnp.int32),
            pltpu.VMEM((PAR_DEV, 32), jnp.int32),
            pltpu.VMEM((PAR_DEV, 32), jnp.int32),
            dma((4,)),
            dma((5,)),
            dma((6,)),
            dma((6,)),
            dma((4,)),
            dma((4,)),
            dma,
            dma,
            dma((4,)),
            dma((4,)),
            dma((3,)),
            dma((3,)),
        ],
        compiler_params=pltpu.CompilerParams(
            has_side_effects=True, vmem_limit_bytes=VMEM_BYTES
        ),
        cost_estimate=pl.CostEstimate(
            flops=5 * 10**9, bytes_accessed=10**7, transcendentals=10**7
        ),
        name="multipole",
    )(
        points[:, 0],
        charges[:, 0],
        near_box,
        near_code,
        send_box,
        far_slot,
        far_direction,
        coarse_source,
        coarse_direction,
        leaf_translate,
        coarse_translate,
        child_to_parent,
        parent_to_child,
        jnp.asarray(surf),
        jnp.asarray(np.ascontiguousarray(surf.T)),
    )


def solution(mesh):
    peers = mesh.shape["boxes"]
    grid = {128: (8, 4, 4), 8: (2, 2, 2)}[peers]
    return jax.shard_map(
        functools.partial(on_device, grid),
        mesh=mesh,
        in_specs=(
            P("boxes", "dirs", None),
            P("boxes", "dirs", None, None),
            P("boxes", None),
            P("boxes", None),
            P("boxes", None),
            P("boxes", None),
            P("boxes", None),
            P("boxes", None),
            P("boxes", None),
            P("dirs", None, None),
            P("dirs", None, None),
            P(),
            P(),
        ),
        out_specs=P("boxes", "dirs", None, None),
        check_vma=False,
    )
```

```python
import functools
import math

import jax
import jax.numpy as jnp
import ml_dtypes
import numpy as np
from jax import lax
from jax.experimental import pallas as pl
from jax.experimental.pallas import tpu as pltpu
from jax.sharding import PartitionSpec as P

PTS = 128
EQ = 128
DIRS = 16
RHS = 4
NEAR = 27
CAP = 16
REACH = 2
HB = 8
PAR_DEV = 4
BOX_DEV = 32
HALF_BOX = 16
WINDOW = 64
FEATURES = 16

wave_number = 3.0
smoothing = 0.0625
sphere_radius = 2.5
golden_turn = 2.399963229728653
four_pi = 12.566370614359172

TURNS = wave_number / (2.0 * math.pi)
SCALE = TURNS * TURNS
COS_TERMS = (0.99995979, -19.73104169, 64.67343118, -82.40355071, 45.64655728)
SIN_TERMS = (6.2830558, -41.33121431, 81.36681533, -74.47800473, 32.78140114)
AMPLITUDE = TURNS / four_pi

VMEM_BYTES = 62 * 1024 * 1024
F32, BF16 = jnp.float32, jnp.bfloat16


def surface_features():
    ordinal = np.arange(EQ).astype(np.float32)
    height = np.float32(1.0) - (np.float32(2.0) * ordinal + np.float32(1.0)) / np.float32(EQ)
    radial = np.sqrt(np.float32(1.0) - height * height)
    angles = ordinal * np.float32(golden_turn)
    surface = np.float32(sphere_radius) * np.stack(
        [radial * np.cos(angles), radial * np.sin(angles), height]
    )
    surface = surface.astype(np.float64)

    def split(values):
        parts = []
        for _ in range(3):
            part = values.astype(ml_dtypes.bfloat16).astype(np.float64)
            parts.append(part)
            values = values - part
        return parts

    coords = [split(-2.0 * SCALE * surface[k]) for k in range(3)]
    square = split(SCALE * ((surface * surface).sum(0) + smoothing))
    one = np.ones(EQ)
    rows = [coords[k][i] for i in range(3) for k in range(3)] + [one] * 3 + square + [0.0 * one]
    return np.stack(rows).astype(ml_dtypes.bfloat16)


def split3(values):
    high = values.astype(BF16).astype(F32)
    rest = values - high
    middle = rest.astype(BF16).astype(F32)
    return [high, middle, rest - middle]


def horner(terms, z):
    total = z * (AMPLITUDE * terms[-1]) + AMPLITUDE * terms[-2]
    for term in terms[-3::-1]:
        total = total * z + AMPLITUDE * term
    return total


def wave(scaled):
    inverse = lax.rsqrt(scaled)
    phase = scaled * inverse
    phase = phase - jnp.round(phase)
    z = phase * phase
    real = inverse * horner(COS_TERMS, z)
    imag = (inverse * phase) * horner(SIN_TERMS, z)
    return real.astype(BF16), imag.astype(BF16)


def source_features(coords):
    square = SCALE * sum(c * c for c in coords)
    one = jnp.ones_like(square)
    return coords * 3 + split3(square) + [one, one, one, jnp.zeros_like(one)]


def target_features(coords):
    square = SCALE * (sum(c * c for c in coords) + smoothing)
    one = jnp.ones_like(square)
    parts = [split3(-2.0 * SCALE * c) for c in coords]
    rows = [parts[k][i] for i in range(3) for k in range(3)]
    return rows + [one, one, one] + split3(square) + [jnp.zeros_like(one)]


def dot(a, b):
    return jnp.dot(a, b, preferred_element_type=F32)


def dot_nt(a, b):
    return lax.dot_general(a, b, (((1,), (1,)), ((), ())), preferred_element_type=F32)


def rows_at(start, step, size=None):
    return pl.ds(pl.multiple_of(start, step), size or step)


def one_hot(condition):
    return jnp.where(condition, 1.0, 0.0).astype(BF16)


def iota(shape, dim):
    return lax.broadcasted_iota(jnp.int32, shape, dim)


def kernel(
    grid,
    points_ref,
    charges_ref,
    near_box_ref,
    near_code_ref,
    send_hbm,
    slot_hbm,
    slot_dir_hbm,
    coarse_source_hbm,
    coarse_dir_hbm,
    leaf_hbm,
    coarse_hbm,
    up_hbm,
    down_hbm,
    surf_x_ref,
    surf_y_ref,
    out_ref,
    pos_ref,
    own_ref,
    dense_ref,
    feature_ref,
    source_ref,
    target_ref,
    leaf_ref,
    coarse_tab_ref,
    up_ref,
    down_ref,
    hot_ref,
    hot_near_ref,
    raised_ref,
    outgoing_ref,
    send_buf,
    send_near,
    recv_buf,
    parent_buf,
    weight_ref,
    coarse_weight_ref,
    cone_ref,
    coarse_cone_ref,
    child_ref,
    local_ref,
    left_ref,
    near_ref,
    far_x_ref,
    far_ref,
    send_ref,
    send_rows_ref,
    slot_ref,
    slot_dir_ref,
    coarse_ref,
    coarse_dir_ref,
    table_sem,
    list_sem,
    pair_send,
    pair_recv,
    halo_send,
    halo_recv,
    all_send,
    all_recv,
    close_send,
    close_recv,
    parent_send,
    parent_recv,
):
    nz, nx, ny = grid
    peers = nz * nx * ny
    blocks = peers // 8
    me = lax.axis_index("boxes")
    core = lax.axis_index("dirs")
    other = 1 - core

    def around(step):
        return lax.rem(me + step + peers, peers)

    def remote(src, dst, send_sem, recv_sem, box_to, core_to):
        return pltpu.make_async_remote_copy(
            src_ref=src,
            dst_ref=dst,
            send_sem=send_sem,
            recv_sem=recv_sem,
            device_id=(box_to, core_to),
            device_id_type=pl.DeviceIdType.MESH,
        )

    list_copies = [
        pltpu.make_async_copy(src, dst, list_sem.at[i])
        for i, (src, dst) in enumerate(
            (
                (send_hbm, send_ref),
                (slot_hbm, slot_ref),
                (slot_dir_hbm, slot_dir_ref),
                (coarse_source_hbm, coarse_ref),
                (coarse_dir_hbm, coarse_dir_ref),
            )
        )
    ]
    for copy in list_copies:
        copy.start()

    points = points_ref[...].astype(F32)
    pos_ref[core, pl.ds(HB, BOX_DEV), :] = jnp.concatenate(
        [points, jnp.zeros((BOX_DEV, 64), F32)], axis=1
    )
    for k in range(3):
        piece = points[:, k * 64 : k * 64 + 64]
        own_ref[k] = jnp.concatenate([piece, piece], axis=1)
    sign = jnp.where(iota((RHS, 128), 1) < 64, 1.0, -1.0)

    def weigh(j, carry):
        q = charges_ref[j].astype(F32)
        both = jnp.concatenate([q * sign, pltpu.roll(q, 64, 1)], axis=0)
        dense_ref[core, HB + j] = jnp.concatenate([both, both], axis=0).astype(BF16)
        return carry

    lax.fori_loop(0, BOX_DEV, weigh, 0, unroll=8)

    pair_copies = [
        remote(
            pos_ref.at[core, pl.ds(HB, BOX_DEV)],
            pos_ref.at[core, pl.ds(HB, BOX_DEV)],
            pair_send.at[0],
            pair_recv.at[0],
            me,
            other,
        ),
        remote(
            dense_ref.at[core, pl.ds(HB, BOX_DEV)],
            dense_ref.at[core, pl.ds(HB, BOX_DEV)],
            pair_send.at[1],
            pair_recv.at[1],
            me,
            other,
        ),
        remote(leaf_hbm, leaf_ref.at[core], pair_send.at[2], pair_recv.at[2], me, other),
        remote(coarse_hbm, coarse_tab_ref.at[core], pair_send.at[3], pair_recv.at[3], me, other),
    ]
    pair_copies[0].start()
    pair_copies[1].start()
    halo_copies = []
    edge = BOX_DEV + HB
    for side, (first, step) in enumerate(((BOX_DEV, 1), (HB, -1))):
        halo_copies.append(
            remote(
                pos_ref.at[core, pl.ds(first, HB)],
                pos_ref.at[core, pl.ds(side * edge, HB)],
                halo_send.at[2 * side],
                halo_recv.at[core],
                around(step),
                side,
            )
        )
        halo_copies.append(
            remote(
                dense_ref.at[core, pl.ds(first, HB)],
                dense_ref.at[core, pl.ds(side * edge, HB)],
                halo_send.at[2 * side + 1],
                halo_recv.at[2 + core],
                around(step),
                side,
            )
        )
    for copy in halo_copies:
        copy.start()
    table_copies = [
        pltpu.make_async_copy(up_hbm, up_ref, table_sem.at[0]),
        pltpu.make_async_copy(coarse_hbm, coarse_tab_ref.at[core], table_sem.at[1]),
        pltpu.make_async_copy(down_hbm, down_ref, table_sem.at[2]),
        pltpu.make_async_copy(leaf_hbm, leaf_ref.at[core], table_sem.at[3]),
    ]
    for copy in table_copies:
        copy.start()
    pair_copies[2].start()
    pair_copies[3].start()

    list_copies[0].wait()
    send_rows_ref[...] = send_ref[...].astype(F32).T
    slot_row = iota((16, CAP), 0)
    slot_lane = iota((16, CAP), 1)
    first_slots = slot_lane == slot_row % 8
    last_slots = slot_lane == slot_row % 8 + 8
    column = iota((16, 64), 1).astype(F32) - (32 * (iota((16, 64), 0) // 8)).astype(F32)

    def slots_of(t, mask):
        row = send_rows_ref[pl.ds(t, 1), :]
        wanted = jnp.sum(jnp.where(mask, row, 0.0), axis=1, keepdims=True)
        return one_hot(wanted == column)

    def mark(t, carry):
        hot_ref[rows_at(t * 16, 16), :] = slots_of(t, first_slots)
        return carry

    lax.fori_loop(0, peers, mark, 0, unroll=8)
    for index in range(5):
        hot_near_ref[pl.ds(index * 16, 16), :] = slots_of(around(index - REACH), last_slots)
    recv_buf[pl.ds((peers + 5) * 16, 48), :] = jnp.zeros((48, 256), BF16)

    def features(first, count):
        coords = [
            jnp.concatenate(
                [
                    pos_ref[0, rows_at(first, HB, count), :][:, k * 64 : k * 64 + 64],
                    pos_ref[1, rows_at(first, HB, count), :][:, k * 64 : k * 64 + 64],
                ],
                axis=1,
            )
            for k in range(3)
        ]
        for f, row in enumerate(source_features(coords)):
            feature_ref[pl.ds(first * FEATURES + f, count, stride=FEATURES), :] = row

        def turn(i, carry):
            j = first + i
            tile = feature_ref[rows_at(j * FEATURES, FEATURES), :]
            turned = tile.T
            blank = jnp.zeros_like(turned)
            source_ref[0, j] = jnp.concatenate([turned, blank], axis=1).astype(BF16)
            source_ref[1, j] = jnp.concatenate([blank, turned], axis=1).astype(BF16)
            return carry

        lax.fori_loop(0, count, turn, 0, unroll=8)

    pair_copies[0].wait_recv()
    features(HB, BOX_DEV)
    pair_copies[1].wait_recv()

    def charges_at(j):
        return jnp.concatenate([dense_ref[0, j], dense_ref[1, j]], axis=1)

    def kernel_tile(y, x):
        parts = []
        for half in range(2):
            pieces = [wave(dot(y[at : at + 32], x)) for at in (half * 64, half * 64 + 32)]
            parts.extend([piece[0] for piece in pieces] + [piece[1] for piece in pieces])
        return jnp.concatenate(parts, axis=0)

    surf_x = surf_x_ref[...]

    def raise_box(b, carry):
        tile = kernel_tile(source_ref[0, HB + b][:, :FEATURES], surf_x)
        raised_ref[rows_at(b * 8, 8), :] = dot(charges_at(HB + b), tile)[:8]
        return carry

    lax.fori_loop(0, BOX_DEV, raise_box, 0, unroll=8)
    outgoing = []
    for r in range(2):
        pieces = [
            raised_ref[pl.ds(2 * core + r + 4 * part, BOX_DEV, stride=8), :] for part in range(2)
        ]
        outgoing.append(jnp.concatenate(pieces, axis=1).astype(BF16))
    outgoing = jnp.concatenate(outgoing, axis=0)
    outgoing_ref[0] = outgoing[:, :128].astype(F32)
    outgoing_ref[1] = outgoing[:, 128:].astype(F32)

    def fill(block, carry):
        rows = rows_at(block * 128, 128)
        send_buf[rows, :] = dot(hot_ref[rows, :], outgoing).astype(BF16)
        return carry

    lax.fori_loop(0, blocks, fill, 0, unroll=min(4, blocks))
    send_near[...] = dot(hot_near_ref[...], outgoing).astype(BF16)

    def leaf_copy(t):
        return remote(
            send_buf.at[rows_at(t * 16, 16)],
            recv_buf.at[rows_at(me * 16, 16)],
            all_send,
            all_recv,
            t,
            core,
        )

    table_copies[0].wait()
    parent = jnp.zeros((8, 256), F32)
    for o in range(8):
        pieces = [outgoing_ref[part, pl.ds(o, 8, stride=8), :] for part in range(2)]
        parent += dot(jnp.concatenate(pieces, axis=1).astype(BF16), up_ref[o])
    mz, mx, my = me // (nx * ny), me // ny % nx, me % ny
    mine = (my * nx + mx) * nz + mz
    parent_buf[rows_at(mine * 16, 16), :] = jnp.concatenate(
        [parent[:, :128], parent[:, 128:]], axis=0
    ).astype(BF16)

    def parent_phase(phase):
        count = (nz, nx, ny)[phase]
        size = (16, 16 * nz, 16 * nz * nx)[phase]
        rows = rows_at((mine * 16) // size * size, size)
        copies = []
        for step in range(1, count):
            if phase == 0:
                to = lax.rem(mz + step, nz) * nx * ny + mx * ny + my
            elif phase == 1:
                to = mz * nx * ny + lax.rem(mx + step, nx) * ny + my
            else:
                to = mz * nx * ny + mx * ny + lax.rem(my + step, ny)
            copies.append(
                remote(
                    parent_buf.at[rows],
                    parent_buf.at[rows],
                    parent_send.at[phase],
                    parent_recv.at[phase],
                    to,
                    core,
                )
            )
        every = pl.ds(0, size * (count - 1))
        total = remote(
            parent_buf.at[every],
            parent_buf.at[every],
            parent_send.at[phase],
            parent_recv.at[phase],
            me,
            other,
        )
        return copies, total

    phases = [parent_phase(phase) for phase in range(3)]
    for copy in phases[0][0]:
        copy.start()

    def send_leaf(step, carry):
        leaf_copy(around(step)).start()
        return carry

    close_copies = []
    for index, step in enumerate((-2, -1, 1, 2)):
        close_copies.append(
            remote(
                send_near.at[pl.ds((step + REACH) * 16, 16)],
                recv_buf.at[pl.ds((peers + REACH - step) * 16, 16)],
                close_send.at[index],
                close_recv.at[index],
                around(step),
                core,
            )
        )
    for copy in close_copies:
        copy.start()
    lax.fori_loop(1, peers, send_leaf, 0)
    recv_buf[rows_at(me * 16, 16), :] = send_buf[rows_at(me * 16, 16), :]
    recv_buf[pl.ds((peers + REACH) * 16, 16), :] = send_near[pl.ds(REACH * 16, 16), :]

    for half in range(2):
        remote(
            pos_ref.at[half, pl.ds(HB, HB)],
            pos_ref.at[half, rows_at(core * edge, HB)],
            halo_send.at[0],
            halo_recv.at[half],
            me,
            other,
        ).wait_recv()
        remote(
            dense_ref.at[half, pl.ds(HB, HB)],
            dense_ref.at[half, pl.ds(core * edge, HB)],
            halo_send.at[1],
            halo_recv.at[2 + half],
            me,
            other,
        ).wait_recv()
    features(core * edge, HB)
    first_box = core * HALF_BOX
    near_rows = rows_at(HB + first_box, HB, HALF_BOX)
    mine_coords = [
        jnp.concatenate(
            [
                pos_ref[0, near_rows, :][:, k * 64 : k * 64 + 64],
                pos_ref[1, near_rows, :][:, k * 64 : k * 64 + 64],
            ],
            axis=1,
        )
        for k in range(3)
    ]
    for code in range(27):
        offset = (2.0 * (code // 9 - 1), 2.0 * (code // 3 % 3 - 1), 2.0 * (code % 3 - 1))
        moved = [c - o for c, o in zip(mine_coords, offset)]
        for f, row in enumerate(target_features(moved)):
            far_x_ref[pl.ds(f, HALF_BOX, stride=FEATURES), :] = row
        for b in range(HALF_BOX):
            target_ref[code * HALF_BOX + b] = far_x_ref[pl.ds(b * FEATURES, FEATURES), :].astype(
                BF16
            )

    upper = iota((16, 256), 0) < 8
    pad = jnp.zeros((FEATURES, PTS), BF16)

    def near_pair_sum(pair, carry):
        b = 2 * pair

        @pl.when(pair == 2)
        def _():
            phases[0][1].wait_recv()
            for copy in phases[1][0]:
                copy.start()

        @pl.when(pair == 4)
        def _():
            phases[1][1].wait_recv()
            for copy in phases[2][0]:
                copy.start()

        total = jnp.zeros((16, 2 * PTS), F32)
        for n in range(NEAR):
            j, code = [], []
            for k in range(2):
                place = near_box_ref[first_box + b + k, n] - me * BOX_DEV + HB
                j.append(place & (WINDOW - 1))
                code.append(near_code_ref[first_box + b + k, n] * HALF_BOX + b + k)
            y = source_ref[0, j[0]] + source_ref[1, j[1]]
            x = jnp.concatenate(
                [
                    jnp.concatenate([target_ref[code[0]], pad], axis=1),
                    jnp.concatenate([pad, target_ref[code[1]]], axis=1),
                ],
                axis=0,
            )
            q = jnp.where(upper, charges_at(j[0]), charges_at(j[1]))
            total = total + dot(q, kernel_tile(y, x))
        near_ref[rows_at((first_box + b) * 8, 16), :] = jnp.concatenate(
            [total[:8, :PTS], total[8:, PTS:]], axis=0
        )
        return carry

    lax.fori_loop(0, HALF_BOX // 2, near_pair_sum, 0)
    near_copy = remote(
        near_ref.at[rows_at(core * 128, 128)],
        near_ref.at[rows_at(core * 128, 128)],
        pair_send.at[4],
        pair_recv.at[4],
        me,
        other,
    )
    near_copy.start()

    lane = iota((HALF_BOX, 128), 1)
    pair_coords = [
        jnp.where(
            lane < 64,
            own_ref[k, pl.ds(0, HALF_BOX, stride=2), :],
            own_ref[k, pl.ds(1, HALF_BOX, stride=2), :],
        )
        for k in range(3)
    ]
    for f, row in enumerate(source_features(pair_coords)):
        far_x_ref[pl.ds(f, HALF_BOX, stride=FEATURES), :] = row
    surf_y = surf_y_ref[...]

    def lower(pair, carry):
        x = far_x_ref[rows_at(pair * FEATURES, FEATURES), :].astype(BF16)
        real, imag = wave(dot(surf_y, x))
        far_ref[rows_at(pair * 256, 256), :] = jnp.concatenate([real, imag], axis=0)
        return carry

    lax.fori_loop(0, HALF_BOX, lower, 0, unroll=8)

    for copy in list_copies[1:]:
        copy.wait()
    head = iota(((blocks + 1) * 16, 128), 0)
    tail = iota((256, 128), 0)
    tail = tail % 128 - 8 * (tail // 128)

    def count_slots(b, carry):
        v = slot_ref[pl.ds(b, 1), :]
        s, c = v >> 4, v & 15
        late = c >= 8
        gap = (s - me + REACH) & (peers - 1)
        high = jnp.where(late, blocks, s >> 3)
        low = jnp.where(late, gap * 16 + c - 8, (s & 7) * 16 + c)
        a = one_hot(head == high * 16 + slot_dir_ref[pl.ds(b, 1), :])
        counts = dot_nt(a, one_hot(tail == low)).astype(BF16)
        for h in range(blocks + 1):
            for r in range(2):
                weight_ref[r, rows_at(b * 16, 16), pl.ds(h * 128, 128)] = counts[
                    h * 16 : h * 16 + 16, r * 128 : r * 128 + 128
                ]
        return carry

    lax.fori_loop(0, BOX_DEV, count_slots, 0, unroll=4)

    coarse_head = iota((blocks * 16, 32), 0)
    coarse_tail = iota((512, 32), 0)
    coarse_tail = coarse_tail % 128 - 4 * (coarse_tail // 128)
    for p in range(PAR_DEV):
        v = coarse_ref[pl.ds(p, 1), :]
        dev, q = v >> 2, v & 3
        dz, dx, dy = dev >> ((nx * ny).bit_length() - 1), dev >> (ny.bit_length() - 1), dev
        place = ((dy & (ny - 1)) * nx + (dx & (nx - 1))) * nz + dz
        a = one_hot(coarse_head == (place >> 3) * 16 + coarse_dir_ref[pl.ds(p, 1), :])
        counts = dot_nt(a, one_hot(coarse_tail == (place & 7) * 16 + q)).astype(BF16)
        for h in range(blocks):
            for part in range(4):
                coarse_weight_ref[part, pl.ds(p * 16, 16), pl.ds(h * 128, 128)] = counts[
                    h * 16 : h * 16 + 16, part * 128 : part * 128 + 128
                ]
    phases[2][1].wait_recv()
    parents = parent_buf[...]
    for part in range(4):
        coarse_cone_ref[part // 2, pl.ds(part % 2 * 64, 64), :] = dot(
            coarse_weight_ref[part], parents
        )
    table_copies[1].wait()
    pair_copies[3].wait_recv()
    coarse_local = jnp.zeros((8, 256), F32)
    for d in range(DIRS):
        pieces = [coarse_cone_ref[part, pl.ds(d, 8, stride=16), :] for part in range(2)]
        coarse_local += dot(
            jnp.concatenate(pieces, axis=1).astype(BF16), coarse_tab_ref[d // 8, d % 8]
        )
    coarse_local = coarse_local.astype(BF16)
    table_copies[2].wait()
    for o in range(8):
        child = dot(coarse_local, down_ref[o])
        for part in range(2):
            child_ref[part, pl.ds(o, 8, stride=8), :] = child[:, part * 128 : part * 128 + 128]

    every = pl.ds(0, (peers - 1) * 16)
    all_copies = remote(send_buf.at[every], recv_buf.at[every], all_send, all_recv, me, other)
    all_copies.wait_recv()
    for copy in close_copies:
        copy.wait_recv()

    def leaf_cones(block, carry):
        rows = rows_at(block * 128, 128)
        received = recv_buf[...]
        for r in range(2):
            cone = dot(weight_ref[r, rows, :], received)
            to = rows_at(r * 512 + block * 128, 128)
            cone_ref[0, to, :] = cone[:, :128]
            cone_ref[1, to, :] = cone[:, 128:]
        return carry

    lax.fori_loop(0, 4, leaf_cones, 0)
    table_copies[3].wait()
    pair_copies[2].wait_recv()
    local = jnp.concatenate([child_ref[0], child_ref[1]], axis=1)
    for d in range(DIRS):
        pieces = [cone_ref[part, pl.ds(d, 64, stride=16), :] for part in range(2)]
        local += dot(jnp.concatenate(pieces, axis=1).astype(BF16), leaf_ref[d // 8, d % 8])
    local_ref[core] = local.astype(BF16)
    local_copy = remote(
        local_ref.at[core], local_ref.at[core], pair_send.at[5], pair_recv.at[5], me, other
    )
    local_copy.start()
    near_copy.wait_recv()
    local_copy.wait_recv()
    for half in range(2):
        for r in range(2):
            piece = local_ref[half, pl.ds(r * BOX_DEV, BOX_DEV), :].astype(F32)
            real, imag = piece[:, :128], piece[:, 128:]
            row = 2 * half + r
            left_ref[0, pl.ds(row, BOX_DEV, stride=8), :] = real
            left_ref[1, pl.ds(row, BOX_DEV, stride=8), :] = -imag
            left_ref[0, pl.ds(row + RHS, BOX_DEV, stride=8), :] = imag
            left_ref[1, pl.ds(row + RHS, BOX_DEV, stride=8), :] = real
    lane = iota((16, 128), 1)
    swap = (iota((16, 128), 0) < 8) == (core == 1)
    low_lane = iota((RHS, 128), 1) < 64

    def finish(pair, carry):
        rows = rows_at(pair * 16, 16)
        left = jnp.concatenate([left_ref[0, rows, :], left_ref[1, rows, :]], axis=1).astype(BF16)
        near = near_ref[rows, :]
        total = dot(left, far_ref[rows_at(pair * 256, 256), :]) + jnp.where(
            swap, pltpu.roll(near, 64, 1), near
        )
        turned = pltpu.roll(total, 64, 1)
        out_ref[2 * pair, 0] = jnp.where(low_lane, total[0:4], turned[4:8]).astype(BF16)
        out_ref[2 * pair + 1, 0] = jnp.where(low_lane, turned[8:12], total[12:16]).astype(BF16)
        return carry

    lax.fori_loop(0, HALF_BOX, finish, 0, unroll=8)

    for copy in pair_copies + halo_copies + close_copies + [near_copy, local_copy]:
        copy.wait_send()
    all_copies.wait_send()
    for phase in range(3):
        phases[phase][1].wait_send()


def on_device(
    grid,
    points,
    charges,
    near_box,
    near_code,
    send_box,
    far_slot,
    far_direction,
    coarse_source,
    coarse_direction,
    leaf_translate,
    coarse_translate,
    child_to_parent,
    parent_to_child,
):
    peers = grid[0] * grid[1] * grid[2]
    blocks = peers // 8
    vmem = pl.BlockSpec(memory_space=pltpu.VMEM)
    smem = pl.BlockSpec(memory_space=pltpu.SMEM)
    hbm = pl.BlockSpec(memory_space=pl.ANY)
    surf = surface_features()
    dma = pltpu.SemaphoreType.DMA
    return pl.pallas_call(
        functools.partial(kernel, grid),
        out_shape=jax.ShapeDtypeStruct((BOX_DEV, 1, RHS, 128), BF16),
        in_specs=[vmem, vmem, smem, smem] + [hbm] * 9 + [vmem, vmem],
        out_specs=vmem,
        scratch_shapes=[
            pltpu.VMEM((2, WINDOW, 256), F32),
            pltpu.VMEM((3, BOX_DEV, 128), F32),
            pltpu.VMEM((2, WINDOW, 16, 128), BF16),
            pltpu.VMEM((WINDOW * FEATURES, 128), F32),
            pltpu.VMEM((2, WINDOW, PTS, 2 * FEATURES), BF16),
            pltpu.VMEM((27 * HALF_BOX, FEATURES, 128), BF16),
            pltpu.VMEM((2, 8, 256, 256), BF16),
            pltpu.VMEM((2, 8, 256, 256), BF16),
            pltpu.VMEM((8, 256, 256), BF16),
            pltpu.VMEM((8, 256, 256), BF16),
            pltpu.VMEM((peers * 16, 64), BF16),
            pltpu.VMEM((5 * 16, 64), BF16),
            pltpu.VMEM((BOX_DEV * 8, 128), F32),
            pltpu.VMEM((2, 64, 128), F32),
            pltpu.VMEM((peers * 16, 256), BF16),
            pltpu.VMEM((5 * 16, 256), BF16),
            pltpu.VMEM(((peers + 8) * 16, 256), BF16),
            pltpu.VMEM((peers * 16, 128), BF16),
            pltpu.VMEM((2, BOX_DEV * DIRS, (blocks + 1) * 128), BF16),
            pltpu.VMEM((4, PAR_DEV * DIRS, blocks * 128), BF16),
            pltpu.VMEM((2, 2 * BOX_DEV * DIRS, 128), F32),
            pltpu.VMEM((2, 2 * PAR_DEV * DIRS, 128), F32),
            pltpu.VMEM((2, 64, 128), F32),
            pltpu.VMEM((2, 64, 256), BF16),
            pltpu.VMEM((2, BOX_DEV * 8, 128), F32),
            pltpu.VMEM((BOX_DEV * 8, 128), F32),
            pltpu.VMEM((HALF_BOX * FEATURES, 128), F32),
            pltpu.VMEM((HALF_BOX * 256, 128), BF16),
            pltpu.VMEM((CAP, peers), jnp.int32),
            pltpu.VMEM((peers, CAP), F32),
            pltpu.VMEM((BOX_DEV, 128), jnp.int32),
            pltpu.VMEM((BOX_DEV, 128), jnp.int32),
            pltpu.VMEM((PAR_DEV, 32), jnp.int32),
            pltpu.VMEM((PAR_DEV, 32), jnp.int32),
            dma((4,)),
            dma((5,)),
            dma((6,)),
            dma((6,)),
            dma((4,)),
            dma((4,)),
            dma,
            dma,
            dma((4,)),
            dma((4,)),
            dma((3,)),
            dma((3,)),
        ],
        compiler_params=pltpu.CompilerParams(
            has_side_effects=True, vmem_limit_bytes=VMEM_BYTES
        ),
        cost_estimate=pl.CostEstimate(
            flops=5 * 10**9, bytes_accessed=10**7, transcendentals=10**7
        ),
        name="multipole",
    )(
        points[:, 0],
        charges[:, 0],
        near_box,
        near_code,
        send_box.T,
        far_slot,
        far_direction,
        coarse_source,
        coarse_direction,
        leaf_translate,
        coarse_translate,
        child_to_parent,
        parent_to_child,
        jnp.asarray(surf),
        jnp.asarray(np.ascontiguousarray(surf.T)),
    )


def solution(mesh):
    peers = mesh.shape["boxes"]
    grid = {128: (8, 4, 4), 8: (2, 2, 2)}[peers]
    return jax.shard_map(
        functools.partial(on_device, grid),
        mesh=mesh,
        in_specs=(
            P("boxes", "dirs", None),
            P("boxes", "dirs", None, None),
            P("boxes", None),
            P("boxes", None),
            P("boxes", None),
            P("boxes", None),
            P("boxes", None),
            P("boxes", None),
            P("boxes", None),
            P("dirs", None, None),
            P("dirs", None, None),
            P(),
            P(),
        ),
        out_specs=P("boxes", "dirs", None, None),
        check_vma=False,
    )
```

```python
import functools
import math

import jax
import jax.numpy as jnp
import ml_dtypes
import numpy as np
from jax import lax
from jax.experimental import pallas as pl
from jax.experimental.pallas import tpu as pltpu
from jax.sharding import PartitionSpec as P

PTS = 128
EQ = 128
DIRS = 16
RHS = 4
NEAR = 27
CAP = 16
REACH = 2
HB = 8
PAR_DEV = 4
BOX_DEV = 32
HALF_BOX = 16
WINDOW = 64
FEATURES = 16

wave_number = 3.0
smoothing = 0.0625
sphere_radius = 2.5
golden_turn = 2.399963229728653
four_pi = 12.566370614359172

TURNS = wave_number / (2.0 * math.pi)
SCALE = TURNS * TURNS
COS_TERMS = (0.99995979, -19.73104169, 64.67343118, -82.40355071, 45.64655728)
SIN_TERMS = (6.2830558, -41.33121431, 81.36681533, -74.47800473, 32.78140114)
AMPLITUDE = TURNS / four_pi

VMEM_BYTES = 62 * 1024 * 1024
F32, BF16 = jnp.float32, jnp.bfloat16


def surface_features():
    ordinal = np.arange(EQ).astype(np.float32)
    height = np.float32(1.0) - (np.float32(2.0) * ordinal + np.float32(1.0)) / np.float32(EQ)
    radial = np.sqrt(np.float32(1.0) - height * height)
    angles = ordinal * np.float32(golden_turn)
    surface = np.float32(sphere_radius) * np.stack(
        [radial * np.cos(angles), radial * np.sin(angles), height]
    )
    surface = surface.astype(np.float64)

    def split(values):
        parts = []
        for _ in range(3):
            part = values.astype(ml_dtypes.bfloat16).astype(np.float64)
            parts.append(part)
            values = values - part
        return parts

    coords = [split(-2.0 * SCALE * surface[k]) for k in range(3)]
    square = split(SCALE * ((surface * surface).sum(0) + smoothing))
    one = np.ones(EQ)
    rows = [coords[k][i] for i in range(3) for k in range(3)] + [one] * 3 + square + [0.0 * one]
    return np.stack(rows).astype(ml_dtypes.bfloat16)


def split3(values):
    high = values.astype(BF16).astype(F32)
    rest = values - high
    middle = rest.astype(BF16).astype(F32)
    return [high, middle, rest - middle]


def horner(terms, z):
    total = z * (AMPLITUDE * terms[-1]) + AMPLITUDE * terms[-2]
    for term in terms[-3::-1]:
        total = total * z + AMPLITUDE * term
    return total


def wave(scaled):
    inverse = lax.rsqrt(scaled)
    phase = scaled * inverse
    phase = phase - jnp.round(phase)
    z = phase * phase
    real = inverse * horner(COS_TERMS, z)
    imag = (inverse * phase) * horner(SIN_TERMS, z)
    return real.astype(BF16), imag.astype(BF16)


def source_features(coords):
    square = SCALE * sum(c * c for c in coords)
    one = jnp.ones_like(square)
    return coords * 3 + split3(square) + [one, one, one, jnp.zeros_like(one)]


def target_features(coords):
    square = SCALE * (sum(c * c for c in coords) + smoothing)
    one = jnp.ones_like(square)
    parts = [split3(-2.0 * SCALE * c) for c in coords]
    rows = [parts[k][i] for i in range(3) for k in range(3)]
    return rows + [one, one, one] + split3(square) + [jnp.zeros_like(one)]


def dot(a, b):
    return jnp.dot(a, b, preferred_element_type=F32)


def dot_nt(a, b):
    return lax.dot_general(a, b, (((1,), (1,)), ((), ())), preferred_element_type=F32)


def rows_at(start, step, size=None):
    return pl.ds(pl.multiple_of(start, step), size or step)


def one_hot(condition):
    return jnp.where(condition, 1.0, 0.0).astype(BF16)


def iota(shape, dim):
    return lax.broadcasted_iota(jnp.int32, shape, dim)


def kernel(
    grid,
    points_ref,
    charges_ref,
    near_box_ref,
    near_code_ref,
    send_hbm,
    slot_hbm,
    slot_dir_hbm,
    coarse_source_hbm,
    coarse_dir_hbm,
    leaf_hbm,
    coarse_hbm,
    up_hbm,
    down_hbm,
    surf_x_ref,
    surf_y_ref,
    out_ref,
    pos_ref,
    own_ref,
    dense_ref,
    feature_ref,
    source_ref,
    target_ref,
    leaf_ref,
    coarse_tab_ref,
    up_ref,
    down_ref,
    hot_ref,
    hot_near_ref,
    raised_ref,
    outgoing_ref,
    send_buf,
    send_near,
    recv_buf,
    parent_buf,
    weight_ref,
    coarse_weight_ref,
    cone_ref,
    coarse_cone_ref,
    child_ref,
    local_ref,
    left_ref,
    near_ref,
    far_x_ref,
    far_ref,
    send_ref,
    send_rows_ref,
    slot_ref,
    slot_dir_ref,
    coarse_ref,
    coarse_dir_ref,
    table_sem,
    list_sem,
    pair_send,
    pair_recv,
    halo_send,
    halo_recv,
    all_send,
    all_recv,
    close_send,
    close_recv,
    parent_send,
    parent_recv,
):
    nz, nx, ny = grid
    peers = nz * nx * ny
    blocks = peers // 8
    me = lax.axis_index("boxes")
    core = lax.axis_index("dirs")
    other = 1 - core

    def around(step):
        return lax.rem(me + step + peers, peers)

    def remote(src, dst, send_sem, recv_sem, box_to, core_to):
        return pltpu.make_async_remote_copy(
            src_ref=src,
            dst_ref=dst,
            send_sem=send_sem,
            recv_sem=recv_sem,
            device_id=(box_to, core_to),
            device_id_type=pl.DeviceIdType.MESH,
        )

    list_copies = [
        pltpu.make_async_copy(src, dst, list_sem.at[i])
        for i, (src, dst) in enumerate(
            (
                (send_hbm, send_ref),
                (slot_hbm, slot_ref),
                (slot_dir_hbm, slot_dir_ref),
                (coarse_source_hbm, coarse_ref),
                (coarse_dir_hbm, coarse_dir_ref),
            )
        )
    ]
    for copy in list_copies:
        copy.start()

    points = points_ref[...].astype(F32)
    pos_ref[core, pl.ds(HB, BOX_DEV), :] = jnp.concatenate(
        [points, jnp.zeros((BOX_DEV, 64), F32)], axis=1
    )
    for k in range(3):
        piece = points[:, k * 64 : k * 64 + 64]
        own_ref[k] = jnp.concatenate([piece, piece], axis=1)
    sign = jnp.where(iota((RHS, 128), 1) < 64, 1.0, -1.0)

    def weigh(j, carry):
        q = charges_ref[j].astype(F32)
        both = jnp.concatenate([q * sign, pltpu.roll(q, 64, 1)], axis=0)
        dense_ref[core, HB + j] = jnp.concatenate([both, both], axis=0).astype(BF16)
        return carry

    lax.fori_loop(0, BOX_DEV, weigh, 0, unroll=8)

    pair_copies = [
        remote(
            pos_ref.at[core, pl.ds(HB, BOX_DEV)],
            pos_ref.at[core, pl.ds(HB, BOX_DEV)],
            pair_send.at[0],
            pair_recv.at[0],
            me,
            other,
        ),
        remote(
            dense_ref.at[core, pl.ds(HB, BOX_DEV)],
            dense_ref.at[core, pl.ds(HB, BOX_DEV)],
            pair_send.at[1],
            pair_recv.at[1],
            me,
            other,
        ),
        remote(leaf_hbm, leaf_ref.at[core], pair_send.at[2], pair_recv.at[2], me, other),
        remote(coarse_hbm, coarse_tab_ref.at[core], pair_send.at[3], pair_recv.at[3], me, other),
    ]
    pair_copies[0].start()
    pair_copies[1].start()
    halo_copies = []
    edge = BOX_DEV + HB
    for side, (first, step) in enumerate(((BOX_DEV, 1), (HB, -1))):
        halo_copies.append(
            remote(
                pos_ref.at[core, pl.ds(first, HB)],
                pos_ref.at[core, pl.ds(side * edge, HB)],
                halo_send.at[2 * side],
                halo_recv.at[core],
                around(step),
                side,
            )
        )
        halo_copies.append(
            remote(
                dense_ref.at[core, pl.ds(first, HB)],
                dense_ref.at[core, pl.ds(side * edge, HB)],
                halo_send.at[2 * side + 1],
                halo_recv.at[2 + core],
                around(step),
                side,
            )
        )
    for copy in halo_copies:
        copy.start()
    table_copies = [
        pltpu.make_async_copy(up_hbm, up_ref, table_sem.at[0]),
        pltpu.make_async_copy(coarse_hbm, coarse_tab_ref.at[core], table_sem.at[1]),
        pltpu.make_async_copy(down_hbm, down_ref, table_sem.at[2]),
        pltpu.make_async_copy(leaf_hbm, leaf_ref.at[core], table_sem.at[3]),
    ]
    for copy in table_copies:
        copy.start()
    pair_copies[2].start()
    pair_copies[3].start()

    list_copies[0].wait()
    send_rows_ref[...] = send_ref[...].astype(F32).T
    slot_row = iota((16, CAP), 0)
    slot_lane = iota((16, CAP), 1)
    first_slots = slot_lane == slot_row % 8
    last_slots = slot_lane == slot_row % 8 + 8
    column = iota((16, 64), 1).astype(F32) - (32 * (iota((16, 64), 0) // 8)).astype(F32)

    def slots_of(t, mask):
        row = send_rows_ref[pl.ds(t, 1), :]
        wanted = jnp.sum(jnp.where(mask, row, 0.0), axis=1, keepdims=True)
        return one_hot(wanted == column)

    def mark(t, carry):
        hot_ref[rows_at(t * 16, 16), :] = slots_of(t, first_slots)
        return carry

    lax.fori_loop(0, peers, mark, 0, unroll=min(16, peers))
    for index in range(5):
        hot_near_ref[pl.ds(index * 16, 16), :] = slots_of(around(index - REACH), last_slots)
    recv_buf[pl.ds((peers + 5) * 16, 48), :] = jnp.zeros((48, 256), BF16)

    def features(first, count):
        coords = [
            jnp.concatenate(
                [
                    pos_ref[0, rows_at(first, HB, count), :][:, k * 64 : k * 64 + 64],
                    pos_ref[1, rows_at(first, HB, count), :][:, k * 64 : k * 64 + 64],
                ],
                axis=1,
            )
            for k in range(3)
        ]
        for f, row in enumerate(source_features(coords)):
            feature_ref[pl.ds(first * FEATURES + f, count, stride=FEATURES), :] = row

        def turn(i, carry):
            j = first + i
            tile = feature_ref[rows_at(j * FEATURES, FEATURES), :]
            turned = tile.T
            blank = jnp.zeros_like(turned)
            source_ref[0, j] = jnp.concatenate([turned, blank], axis=1).astype(BF16)
            source_ref[1, j] = jnp.concatenate([blank, turned], axis=1).astype(BF16)
            return carry

        lax.fori_loop(0, count, turn, 0, unroll=8)

    pair_copies[0].wait_recv()
    features(HB, BOX_DEV)
    pair_copies[1].wait_recv()

    def charges_at(j):
        return jnp.concatenate([dense_ref[0, j], dense_ref[1, j]], axis=1)

    def kernel_tile(y, x):
        parts = []
        for half in range(2):
            pieces = [wave(dot(y[at : at + 32], x)) for at in (half * 64, half * 64 + 32)]
            parts.extend([piece[0] for piece in pieces] + [piece[1] for piece in pieces])
        return jnp.concatenate(parts, axis=0)

    surf_x = surf_x_ref[...]

    def raise_box(b, carry):
        tile = kernel_tile(source_ref[0, HB + b][:, :FEATURES], surf_x)
        raised_ref[rows_at(b * 8, 8), :] = dot(charges_at(HB + b), tile)[:8]
        return carry

    lax.fori_loop(0, BOX_DEV, raise_box, 0, unroll=16)
    outgoing = []
    for r in range(2):
        pieces = [
            raised_ref[pl.ds(2 * core + r + 4 * part, BOX_DEV, stride=8), :] for part in range(2)
        ]
        outgoing.append(jnp.concatenate(pieces, axis=1).astype(BF16))
    outgoing = jnp.concatenate(outgoing, axis=0)
    outgoing_ref[0] = outgoing[:, :128].astype(F32)
    outgoing_ref[1] = outgoing[:, 128:].astype(F32)

    def fill(block, carry):
        rows = rows_at(block * 128, 128)
        send_buf[rows, :] = dot(hot_ref[rows, :], outgoing).astype(BF16)
        return carry

    lax.fori_loop(0, blocks, fill, 0, unroll=blocks)
    send_near[...] = dot(hot_near_ref[...], outgoing).astype(BF16)

    def leaf_copy(t):
        return remote(
            send_buf.at[rows_at(t * 16, 16)],
            recv_buf.at[rows_at(me * 16, 16)],
            all_send,
            all_recv,
            t,
            core,
        )

    table_copies[0].wait()
    parent = jnp.zeros((8, 256), F32)
    for o in range(8):
        pieces = [outgoing_ref[part, pl.ds(o, 8, stride=8), :] for part in range(2)]
        parent += dot(jnp.concatenate(pieces, axis=1).astype(BF16), up_ref[o])
    mz, mx, my = me // (nx * ny), me // ny % nx, me % ny
    mine = (my * nx + mx) * nz + mz
    parent_buf[rows_at(mine * 16, 16), :] = jnp.concatenate(
        [parent[:, :128], parent[:, 128:]], axis=0
    ).astype(BF16)

    def parent_phase(phase):
        count = (nz, nx, ny)[phase]
        size = (16, 16 * nz, 16 * nz * nx)[phase]
        rows = rows_at((mine * 16) // size * size, size)
        copies = []
        for step in range(1, count):
            if phase == 0:
                to = lax.rem(mz + step, nz) * nx * ny + mx * ny + my
            elif phase == 1:
                to = mz * nx * ny + lax.rem(mx + step, nx) * ny + my
            else:
                to = mz * nx * ny + mx * ny + lax.rem(my + step, ny)
            copies.append(
                remote(
                    parent_buf.at[rows],
                    parent_buf.at[rows],
                    parent_send.at[phase],
                    parent_recv.at[phase],
                    to,
                    core,
                )
            )
        every = pl.ds(0, size * (count - 1))
        total = remote(
            parent_buf.at[every],
            parent_buf.at[every],
            parent_send.at[phase],
            parent_recv.at[phase],
            me,
            other,
        )
        return copies, total

    phases = [parent_phase(phase) for phase in range(3)]
    for copy in phases[0][0]:
        copy.start()

    def send_leaf(step, carry):
        leaf_copy(around(step)).start()
        return carry

    close_copies = []
    for index, step in enumerate((-2, -1, 1, 2)):
        close_copies.append(
            remote(
                send_near.at[pl.ds((step + REACH) * 16, 16)],
                recv_buf.at[pl.ds((peers + REACH - step) * 16, 16)],
                close_send.at[index],
                close_recv.at[index],
                around(step),
                core,
            )
        )
    for copy in close_copies:
        copy.start()
    lax.fori_loop(1, peers, send_leaf, 0)
    recv_buf[rows_at(me * 16, 16), :] = send_buf[rows_at(me * 16, 16), :]
    recv_buf[pl.ds((peers + REACH) * 16, 16), :] = send_near[pl.ds(REACH * 16, 16), :]

    for half in range(2):
        remote(
            pos_ref.at[half, pl.ds(HB, HB)],
            pos_ref.at[half, rows_at(core * edge, HB)],
            halo_send.at[0],
            halo_recv.at[half],
            me,
            other,
        ).wait_recv()
        remote(
            dense_ref.at[half, pl.ds(HB, HB)],
            dense_ref.at[half, pl.ds(core * edge, HB)],
            halo_send.at[1],
            halo_recv.at[2 + half],
            me,
            other,
        ).wait_recv()
    features(core * edge, HB)
    first_box = core * HALF_BOX
    near_rows = rows_at(HB + first_box, HB, HALF_BOX)
    mine_coords = [
        jnp.concatenate(
            [
                pos_ref[0, near_rows, :][:, k * 64 : k * 64 + 64],
                pos_ref[1, near_rows, :][:, k * 64 : k * 64 + 64],
            ],
            axis=1,
        )
        for k in range(3)
    ]
    for code in range(27):
        offset = (2.0 * (code // 9 - 1), 2.0 * (code // 3 % 3 - 1), 2.0 * (code % 3 - 1))
        moved = [c - o for c, o in zip(mine_coords, offset)]
        for f, row in enumerate(target_features(moved)):
            far_x_ref[pl.ds(f, HALF_BOX, stride=FEATURES), :] = row
        for b in range(HALF_BOX):
            target_ref[code * HALF_BOX + b] = far_x_ref[pl.ds(b * FEATURES, FEATURES), :].astype(
                BF16
            )

    upper = iota((16, 256), 0) < 8
    pad = jnp.zeros((FEATURES, PTS), BF16)

    def near_pair_sum(pair, carry):
        b = 2 * pair

        @pl.when(pair == 2)
        def _():
            phases[0][1].wait_recv()
            for copy in phases[1][0]:
                copy.start()

        @pl.when(pair == 4)
        def _():
            phases[1][1].wait_recv()
            for copy in phases[2][0]:
                copy.start()

        total = jnp.zeros((16, 2 * PTS), F32)
        for n in range(NEAR):
            j, code = [], []
            for k in range(2):
                place = near_box_ref[first_box + b + k, n] - me * BOX_DEV + HB
                j.append(place & (WINDOW - 1))
                code.append(near_code_ref[first_box + b + k, n] * HALF_BOX + b + k)
            y = source_ref[0, j[0]] + source_ref[1, j[1]]
            x = jnp.concatenate(
                [
                    jnp.concatenate([target_ref[code[0]], pad], axis=1),
                    jnp.concatenate([pad, target_ref[code[1]]], axis=1),
                ],
                axis=0,
            )
            q = jnp.where(upper, charges_at(j[0]), charges_at(j[1]))
            total = total + dot(q, kernel_tile(y, x))
        near_ref[rows_at((first_box + b) * 8, 16), :] = jnp.concatenate(
            [total[:8, :PTS], total[8:, PTS:]], axis=0
        )
        return carry

    lax.fori_loop(0, HALF_BOX // 2, near_pair_sum, 0)
    near_copy = remote(
        near_ref.at[rows_at(core * 128, 128)],
        near_ref.at[rows_at(core * 128, 128)],
        pair_send.at[4],
        pair_recv.at[4],
        me,
        other,
    )
    near_copy.start()

    lane = iota((HALF_BOX, 128), 1)
    pair_coords = [
        jnp.where(
            lane < 64,
            own_ref[k, pl.ds(0, HALF_BOX, stride=2), :],
            own_ref[k, pl.ds(1, HALF_BOX, stride=2), :],
        )
        for k in range(3)
    ]
    for f, row in enumerate(source_features(pair_coords)):
        far_x_ref[pl.ds(f, HALF_BOX, stride=FEATURES), :] = row
    surf_y = surf_y_ref[...]

    def lower(pair, carry):
        x = far_x_ref[rows_at(pair * FEATURES, FEATURES), :].astype(BF16)
        real, imag = wave(dot(surf_y, x))
        far_ref[rows_at(pair * 256, 256), :] = jnp.concatenate([real, imag], axis=0)
        return carry

    lax.fori_loop(0, HALF_BOX, lower, 0, unroll=16)

    for copy in list_copies[1:]:
        copy.wait()
    head = iota(((blocks + 1) * 16, 128), 0)
    tail = iota((256, 128), 0)
    tail = tail % 128 - 8 * (tail // 128)

    def count_slots(b, carry):
        v = slot_ref[pl.ds(b, 1), :]
        s, c = v >> 4, v & 15
        late = c >= 8
        gap = (s - me + REACH) & (peers - 1)
        high = jnp.where(late, blocks, s >> 3)
        low = jnp.where(late, gap * 16 + c - 8, (s & 7) * 16 + c)
        a = one_hot(head == high * 16 + slot_dir_ref[pl.ds(b, 1), :])
        counts = dot_nt(a, one_hot(tail == low)).astype(BF16)
        for h in range(blocks + 1):
            for r in range(2):
                weight_ref[r, rows_at(b * 16, 16), pl.ds(h * 128, 128)] = counts[
                    h * 16 : h * 16 + 16, r * 128 : r * 128 + 128
                ]
        return carry

    lax.fori_loop(0, BOX_DEV, count_slots, 0, unroll=8)

    coarse_head = iota((blocks * 16, 32), 0)
    coarse_tail = iota((512, 32), 0)
    coarse_tail = coarse_tail % 128 - 4 * (coarse_tail // 128)
    for p in range(PAR_DEV):
        v = coarse_ref[pl.ds(p, 1), :]
        dev, q = v >> 2, v & 3
        dz, dx, dy = dev >> ((nx * ny).bit_length() - 1), dev >> (ny.bit_length() - 1), dev
        place = ((dy & (ny - 1)) * nx + (dx & (nx - 1))) * nz + dz
        a = one_hot(coarse_head == (place >> 3) * 16 + coarse_dir_ref[pl.ds(p, 1), :])
        counts = dot_nt(a, one_hot(coarse_tail == (place & 7) * 16 + q)).astype(BF16)
        for h in range(blocks):
            for part in range(4):
                coarse_weight_ref[part, pl.ds(p * 16, 16), pl.ds(h * 128, 128)] = counts[
                    h * 16 : h * 16 + 16, part * 128 : part * 128 + 128
                ]
    phases[2][1].wait_recv()
    parents = parent_buf[...]
    for part in range(4):
        coarse_cone_ref[part // 2, pl.ds(part % 2 * 64, 64), :] = dot(
            coarse_weight_ref[part], parents
        )
    table_copies[1].wait()
    pair_copies[3].wait_recv()
    coarse_local = jnp.zeros((8, 256), F32)
    for d in range(DIRS):
        pieces = [coarse_cone_ref[part, pl.ds(d, 8, stride=16), :] for part in range(2)]
        coarse_local += dot(
            jnp.concatenate(pieces, axis=1).astype(BF16), coarse_tab_ref[d // 8, d % 8]
        )
    coarse_local = coarse_local.astype(BF16)
    table_copies[2].wait()
    for o in range(8):
        child = dot(coarse_local, down_ref[o])
        for part in range(2):
            child_ref[part, pl.ds(o, 8, stride=8), :] = child[:, part * 128 : part * 128 + 128]

    every = pl.ds(0, (peers - 1) * 16)
    all_copies = remote(send_buf.at[every], recv_buf.at[every], all_send, all_recv, me, other)
    all_copies.wait_recv()
    for copy in close_copies:
        copy.wait_recv()

    def leaf_cones(block, carry):
        rows = rows_at(block * 128, 128)
        received = recv_buf[...]
        for r in range(2):
            cone = dot(weight_ref[r, rows, :], received)
            to = rows_at(r * 512 + block * 128, 128)
            cone_ref[0, to, :] = cone[:, :128]
            cone_ref[1, to, :] = cone[:, 128:]
        return carry

    lax.fori_loop(0, 4, leaf_cones, 0)
    table_copies[3].wait()
    pair_copies[2].wait_recv()
    local = jnp.concatenate([child_ref[0], child_ref[1]], axis=1)
    for d in range(DIRS):
        pieces = [cone_ref[part, pl.ds(d, 64, stride=16), :] for part in range(2)]
        local += dot(jnp.concatenate(pieces, axis=1).astype(BF16), leaf_ref[d // 8, d % 8])
    local_ref[core] = local.astype(BF16)
    local_copy = remote(
        local_ref.at[core], local_ref.at[core], pair_send.at[5], pair_recv.at[5], me, other
    )
    local_copy.start()
    near_copy.wait_recv()
    local_copy.wait_recv()
    for half in range(2):
        for r in range(2):
            piece = local_ref[half, pl.ds(r * BOX_DEV, BOX_DEV), :].astype(F32)
            real, imag = piece[:, :128], piece[:, 128:]
            row = 2 * half + r
            left_ref[0, pl.ds(row, BOX_DEV, stride=8), :] = real
            left_ref[1, pl.ds(row, BOX_DEV, stride=8), :] = -imag
            left_ref[0, pl.ds(row + RHS, BOX_DEV, stride=8), :] = imag
            left_ref[1, pl.ds(row + RHS, BOX_DEV, stride=8), :] = real
    lane = iota((16, 128), 1)
    swap = (iota((16, 128), 0) < 8) == (core == 1)
    low_lane = iota((RHS, 128), 1) < 64

    def finish(pair, carry):
        rows = rows_at(pair * 16, 16)
        left = jnp.concatenate([left_ref[0, rows, :], left_ref[1, rows, :]], axis=1).astype(BF16)
        near = near_ref[rows, :]
        total = dot(left, far_ref[rows_at(pair * 256, 256), :]) + jnp.where(
            swap, pltpu.roll(near, 64, 1), near
        )
        turned = pltpu.roll(total, 64, 1)
        out_ref[2 * pair, 0] = jnp.where(low_lane, total[0:4], turned[4:8]).astype(BF16)
        out_ref[2 * pair + 1, 0] = jnp.where(low_lane, turned[8:12], total[12:16]).astype(BF16)
        return carry

    lax.fori_loop(0, HALF_BOX, finish, 0, unroll=16)

    for copy in pair_copies + halo_copies + close_copies + [near_copy, local_copy]:
        copy.wait_send()
    all_copies.wait_send()
    for phase in range(3):
        phases[phase][1].wait_send()


def on_device(
    grid,
    points,
    charges,
    near_box,
    near_code,
    send_box,
    far_slot,
    far_direction,
    coarse_source,
    coarse_direction,
    leaf_translate,
    coarse_translate,
    child_to_parent,
    parent_to_child,
):
    peers = grid[0] * grid[1] * grid[2]
    blocks = peers // 8
    vmem = pl.BlockSpec(memory_space=pltpu.VMEM)
    smem = pl.BlockSpec(memory_space=pltpu.SMEM)
    hbm = pl.BlockSpec(memory_space=pl.ANY)
    surf = surface_features()
    dma = pltpu.SemaphoreType.DMA
    return pl.pallas_call(
        functools.partial(kernel, grid),
        out_shape=jax.ShapeDtypeStruct((BOX_DEV, 1, RHS, 128), BF16),
        in_specs=[vmem, vmem, smem, smem] + [hbm] * 9 + [vmem, vmem],
        out_specs=vmem,
        scratch_shapes=[
            pltpu.VMEM((2, WINDOW, 256), F32),
            pltpu.VMEM((3, BOX_DEV, 128), F32),
            pltpu.VMEM((2, WINDOW, 16, 128), BF16),
            pltpu.VMEM((WINDOW * FEATURES, 128), F32),
            pltpu.VMEM((2, WINDOW, PTS, 2 * FEATURES), BF16),
            pltpu.VMEM((27 * HALF_BOX, FEATURES, 128), BF16),
            pltpu.VMEM((2, 8, 256, 256), BF16),
            pltpu.VMEM((2, 8, 256, 256), BF16),
            pltpu.VMEM((8, 256, 256), BF16),
            pltpu.VMEM((8, 256, 256), BF16),
            pltpu.VMEM((peers * 16, 64), BF16),
            pltpu.VMEM((5 * 16, 64), BF16),
            pltpu.VMEM((BOX_DEV * 8, 128), F32),
            pltpu.VMEM((2, 64, 128), F32),
            pltpu.VMEM((peers * 16, 256), BF16),
            pltpu.VMEM((5 * 16, 256), BF16),
            pltpu.VMEM(((peers + 8) * 16, 256), BF16),
            pltpu.VMEM((peers * 16, 128), BF16),
            pltpu.VMEM((2, BOX_DEV * DIRS, (blocks + 1) * 128), BF16),
            pltpu.VMEM((4, PAR_DEV * DIRS, blocks * 128), BF16),
            pltpu.VMEM((2, 2 * BOX_DEV * DIRS, 128), F32),
            pltpu.VMEM((2, 2 * PAR_DEV * DIRS, 128), F32),
            pltpu.VMEM((2, 64, 128), F32),
            pltpu.VMEM((2, 64, 256), BF16),
            pltpu.VMEM((2, BOX_DEV * 8, 128), F32),
            pltpu.VMEM((BOX_DEV * 8, 128), F32),
            pltpu.VMEM((HALF_BOX * FEATURES, 128), F32),
            pltpu.VMEM((HALF_BOX * 256, 128), BF16),
            pltpu.VMEM((CAP, peers), jnp.int32),
            pltpu.VMEM((peers, CAP), F32),
            pltpu.VMEM((BOX_DEV, 128), jnp.int32),
            pltpu.VMEM((BOX_DEV, 128), jnp.int32),
            pltpu.VMEM((PAR_DEV, 32), jnp.int32),
            pltpu.VMEM((PAR_DEV, 32), jnp.int32),
            dma((4,)),
            dma((5,)),
            dma((6,)),
            dma((6,)),
            dma((4,)),
            dma((4,)),
            dma,
            dma,
            dma((4,)),
            dma((4,)),
            dma((3,)),
            dma((3,)),
        ],
        compiler_params=pltpu.CompilerParams(
            has_side_effects=True, vmem_limit_bytes=VMEM_BYTES
        ),
        cost_estimate=pl.CostEstimate(
            flops=5 * 10**9, bytes_accessed=10**7, transcendentals=10**7
        ),
        name="multipole",
    )(
        points[:, 0],
        charges[:, 0],
        near_box,
        near_code,
        send_box.T,
        far_slot,
        far_direction,
        coarse_source,
        coarse_direction,
        leaf_translate,
        coarse_translate,
        child_to_parent,
        parent_to_child,
        jnp.asarray(surf),
        jnp.asarray(np.ascontiguousarray(surf.T)),
    )


def solution(mesh):
    peers = mesh.shape["boxes"]
    grid = {128: (8, 4, 4), 8: (2, 2, 2)}[peers]
    return jax.shard_map(
        functools.partial(on_device, grid),
        mesh=mesh,
        in_specs=(
            P("boxes", "dirs", None),
            P("boxes", "dirs", None, None),
            P("boxes", None),
            P("boxes", None),
            P("boxes", None),
            P("boxes", None),
            P("boxes", None),
            P("boxes", None),
            P("boxes", None),
            P("dirs", None, None),
            P("dirs", None, None),
            P(),
            P(),
        ),
        out_specs=P("boxes", "dirs", None, None),
        check_vma=False,
    )
```
